256 devices in a mesh: grav: 8 (over y, z_lo), cross: 32 (over z_hi, x, core).
Axes of the slice: x: 4, y: 4, z: 8 (z_hi: 4, z_lo: 2; z = z_hi * 2 + z_lo), core: 2. Of those that a mesh axis runs over, the one named last changes fastest.
Arguments:
- drift: float32 [3, 64, 262144], P(None, None, ('grav', 'cross')), may hold values from -6 to 6
- warm: float32 [3, 64, 262144], P(None, None, ('grav', 'cross')), may hold values from -6 to 6
- gap: float32 [3, 64, 262144], P(None, None, ('grav', 'cross')), may hold values from -6 to 6
- mobility: bfloat16 [8, 192, 192], replicated, may hold values from -0.3125 to 0.3125
- near_list: int32 [4, 32768], P(None, ('grav', 'cross')), may hold values from 0 to 1023, as said below
- send_slot: int32 [4, 8192], P(None, ('grav', 'cross')), may hold values from 0 to 1023, as said below
- land_slot: int32 [4, 8192], P(None, ('grav', 'cross')), may hold values from 0 to 1023, as said below
- contacts: int32 [3, 524288], P(None, ('grav', 'cross')), may hold values from 0 to 1535, as said below
- live: int32 [256], P(('grav', 'cross')), may hold values from 256 to 2048, as said below
Outputs:
- impulse: float32 [3, 64, 262144], P(None, None, ('grav', 'cross'))
- contact_rate: float32 [3, 64, 262144], P(None, None, ('grav', 'cross'))
The draws below stay inside these ranges and needn't reach their ends.
Inputs may be any that keep to these rules, and one draw needn't show every extreme that they name: `near_list`: per brick, the 512 slots are distinct and none is a send or landing slot. `send_slot`: per brick, the 128 slots are distinct and none is a landing slot. `land_slot`: per brick, the 128 slots are distinct. `contacts`: row 0 is a slot of the brick's own fibres; row 1 is an extended column, never equal to row 0; row 2 a block kind below 8. Bricks of the lowest gravity layer hold 2048 live contacts; every brick holds at least 256.
All inputs are finite; a program needn't handle non-finite values.
Results may differ from the reference program's by a relative error of at most 0.0032.
Values sent between devices are 32-bit elements; how exact they have to be, the bound alone decides.
No kernel may reach another device: no remote copies, remote signals or barrier semaphores. Data moves between devices by JAX's collectives and lax.ppermute only.
A program may use at most 64 MiB of HBM per device.

```python
import jax
import jax.numpy as jnp
from jax import lax

SEG = 64
NBLK = 8
SWEEPS = 3
FIB = 1024
NEAR = 128
MIG = 32
CON = 2048
FIBRES = 262144
N_GRAV = 8
N_CROSS = 32


def slot_table(key):
    key = jax.random.fold_in(key, 101)
    bricks = N_GRAV * N_CROSS
    keys = jax.random.split(key, bricks)
    return jax.vmap(lambda single: jax.random.permutation(single, FIB))(keys).astype(jnp.int32)


def to_global(block, rows, width):
    bricks = N_GRAV * N_CROSS
    return block.reshape(bricks, rows, width).transpose(1, 0, 2).reshape(rows, bricks * width)


def draw_near_list(key, part):
    table = slot_table(key)
    return to_global(table[:, :4 * NEAR], 4, NEAR)


def draw_send_slot(key, part):
    table = slot_table(key)
    return to_global(table[:, 4 * NEAR:4 * NEAR + 4 * MIG], 4, MIG)


def draw_land_slot(key, part):
    table = slot_table(key)
    return to_global(table[:, 4 * NEAR + 4 * MIG:4 * NEAR + 8 * MIG], 4, MIG)


def draw_contacts(key, part):
    key = jax.random.fold_in(key, 7)
    first_key, second_key, kind_key = jax.random.split(key, 3)
    total = N_GRAV * N_CROSS * CON
    span = FIB + 4 * NEAR
    first = jax.random.randint(first_key, (total,), 0, FIB, dtype=jnp.int32)
    offset = jax.random.randint(second_key, (total,), 1, span, dtype=jnp.int32)
    second = (first + offset) % span
    kinds = jax.random.randint(kind_key, (total,), 0, NBLK, dtype=jnp.int32)
    return jnp.stack([first, second, kinds], axis=0).astype(jnp.int32)


def draw_live(key, part):
    key = jax.random.fold_in(key, 5)
    bricks = N_GRAV * N_CROSS
    layer = jnp.arange(bricks, dtype=jnp.int32) // N_CROSS
    dropped = jax.random.randint(key, (bricks,), CON // 2, 7 * CON // 8 + 1, dtype=jnp.int32)
    return (CON - layer * dropped // max(N_GRAV - 1, 1)).astype(jnp.int32)


def block_scale(stream_key, extent, cuts, low, top_value):
    factor_of = 1.0
    for dim, parts in cuts:
        heights = jax.random.uniform(jax.random.fold_in(jax.random.fold_in(stream_key, 6), dim), (parts,), jnp.float32, low / len(cuts), top_value / len(cuts))
        factor_of = factor_of * jnp.repeat(jnp.exp(heights), extent[dim] // parts).reshape((-1,) + (1,) * (len(extent) - 1 - dim))
    return factor_of


def gaussian(rng, dims, spread, most, cuts=(), held_as=jnp.bfloat16):
    loudness = block_scale(rng, dims, cuts, -0.22, 0.18) if cuts else 1.0
    drawn = jax.random.normal(rng, dims, jnp.float32) * spread * loudness
    return jnp.minimum(jnp.maximum(drawn, -most), most).astype(held_as)


def setup_inputs(seed: int = 0) -> dict:
    arg_keys = jax.random.split(jax.random.key(seed), 10)
    return {
        "drift": gaussian(arg_keys[0], (3, SEG, FIBRES), 1.0, 6.0, ((2, 256),), jnp.float32),
        "warm": gaussian(arg_keys[1], (3, SEG, FIBRES), 1.0, 6.0, ((2, 256),), jnp.float32),
        "gap": gaussian(arg_keys[2], (3, SEG, FIBRES), 1.0, 6.0, ((2, 256),), jnp.float32),
        "mobility": gaussian(arg_keys[3], (NBLK, 3 * SEG, 3 * SEG), (6 * SEG) ** -0.5, 0.3125),
        "near_list": draw_near_list(jax.random.fold_in(arg_keys[9], 71), 0),
        "send_slot": draw_send_slot(jax.random.fold_in(arg_keys[9], 71), 0),
        "land_slot": draw_land_slot(jax.random.fold_in(arg_keys[9], 71), 0),
        "contacts": draw_contacts(jax.random.fold_in(arg_keys[9], 71), 0),
        "live": draw_live(jax.random.fold_in(arg_keys[9], 71), 0),
    }


OMEGA = 0.5
FRICTION = 0.4


def per_brick(field):
    bricks = N_GRAV * N_CROSS
    return field.reshape(3 * SEG, bricks, FIB).transpose(1, 0, 2)


def per_brick_int(table, rows, width):
    bricks = N_GRAV * N_CROSS
    return table.reshape(rows, bricks, width).transpose(1, 0, 2)


def neighbours(sent):
    bricks = N_GRAV * N_CROSS
    shaped = sent.reshape((N_GRAV, N_CROSS) + sent.shape[1:])
    empty = jnp.zeros_like(shaped[:1, :, 1])
    below = jnp.concatenate([empty, shaped[:-1, :, 1]], axis=0)
    above = jnp.concatenate([shaped[1:, :, 0], empty], axis=0)
    left = jnp.roll(shaped[:, :, 3], 1, axis=1)
    right = jnp.roll(shaped[:, :, 2], -1, axis=1)
    joined = jnp.stack([below, above, left, right], axis=2)
    return joined.reshape((bricks,) + sent.shape[1:])


def place(block, sends, lands, arrived):
    width = block.shape[0]
    block = block.at[:, sends.reshape(-1)].set(0.0)
    return block.at[:, lands.reshape(-1)].set(arrived.transpose(1, 0, 2).reshape(width, -1))


def project(trial):
    shaped = trial.reshape(trial.shape[0], 3, SEG, FIB)
    normal = jnp.maximum(shaped[:, 0], 0.0)
    bound = FRICTION * normal
    tangent = jnp.minimum(jnp.maximum(shaped[:, 1:], -bound[:, None]), bound[:, None])
    return jnp.concatenate([normal[:, None], tangent], axis=1).reshape(trial.shape)


def reference(drift, warm, gap, mobility, near_list, send_slot, land_slot, contacts, live):
    width = 3 * SEG
    drift_b = per_brick(drift)
    warm_b = per_brick(warm)
    gap_b = per_brick(gap)
    near_b = per_brick_int(near_list, 4, NEAR)
    send_b = per_brick_int(send_slot, 4, MIG)
    land_b = per_brick_int(land_slot, 4, MIG)
    contact_b = per_brick_int(contacts, 3, CON)
    leaving = jax.vmap(lambda block, slots: block[:, slots].transpose(1, 0, 2))(warm_b, send_b)
    arrived = neighbours(leaving)
    lam = jax.vmap(place)(warm_b, send_b, land_b, arrived)
    mobility_wide = mobility.astype(jnp.float32)

    def brick_rates(items):
        velocity, halo, pattern, count = items
        extended = jnp.concatenate([velocity, halo], axis=1)
        first, second, kind = pattern[0], pattern[1], pattern[2]
        mask = (jnp.arange(CON) < count).astype(jnp.float32)
        diff = ((extended[:, first] - extended[:, second]) * mask).astype(jnp.bfloat16)
        diff = lax.optimization_barrier(diff).astype(jnp.float32)
        rate = jnp.zeros((width, CON), jnp.float32)
        for which in range(NBLK):
            chosen = diff * (kind == which).astype(jnp.float32)[None, :]
            rate = rate + jnp.dot(mobility_wide[which], chosen, precision=lax.Precision.HIGHEST)
        return jnp.zeros((width, FIB), jnp.float32).at[:, first].add(rate)

    rates = jnp.zeros_like(lam)
    for repeat in range(SWEEPS):
        velocity = drift_b + lam
        near_vel = jax.vmap(lambda block, slots: block[:, slots].transpose(1, 0, 2))(velocity, near_b)
        halo = neighbours(near_vel)
        halo = halo.transpose(0, 2, 1, 3).reshape(halo.shape[0], width, 4 * NEAR)
        rates = lax.map(brick_rates, (velocity, halo, contact_b, live))
        lam = project(lam - OMEGA * (rates + gap_b))

    def back(field):
        return field.transpose(1, 0, 2).reshape(3, SEG, -1)

    return back(lam), back(rates)
```

```python
import functools

import jax
import jax.numpy as jnp
from jax import lax
from jax.experimental import pallas as pl
from jax.experimental.pallas import tpu as pltpu
from jax.sharding import PartitionSpec as P

SWEEPS = 3
OMEGA = 0.5
FRICTION = 0.4
LANES = 128
CHUNK = 256
VMEM_LIMIT = 56 * 1024 * 1024
F32 = jnp.float32
BF16 = jnp.bfloat16


def ring(x, axis, by):
    count = lax.axis_size(axis)
    return lax.ppermute(x, axis, [(i, (i + by) % count) for i in range(count)])


def exchange(sent):
    left = ring(sent[3], "cross", 1)
    right = ring(sent[2], "cross", -1)
    below = ring(sent[1], "grav", 1)
    above = ring(sent[0], "grav", -1)
    return below, above, left, right


def split(x, parts):
    out = []
    for _ in range(parts - 1):
        part = x.astype(BF16)
        out.append(part)
        x = x - part.astype(F32)
    out.append(x.astype(BF16))
    return jnp.concatenate(out, axis=0)


def join(y, parts):
    rows = y.shape[0] // parts
    total = y[(parts - 1) * rows:]
    for i in range(parts - 2, -1, -1):
        total = total + y[i * rows:(i + 1) * rows]
    return total


def dot(a, b):
    return jnp.dot(a, b, preferred_element_type=F32)


def iota(shape, dim):
    return lax.broadcasted_iota(jnp.int32, shape, dim)


def onehot(flag):
    return jnp.where(flag, 1.0, 0.0).astype(BF16)


def column(row):
    size = row.shape[1]
    eye = iota((size, size), 0) == iota((size, size), 1)
    return jnp.sum(jnp.where(eye, row.astype(F32), 0.0), axis=1, keepdims=True).astype(jnp.int32)


def row_of(table):
    return jnp.concatenate([table[i:i + 1] for i in range(table.shape[0])], axis=1)


def project(trial):
    third = trial.shape[0] // 3
    normal = jnp.maximum(trial[:third], 0.0)
    bound = FRICTION * normal
    first = jnp.minimum(jnp.maximum(trial[third:2 * third], -bound), bound)
    second = jnp.minimum(jnp.maximum(trial[2 * third:], -bound), bound)
    return jnp.concatenate([normal, first, second], axis=0)


def lane_group(rows):
    return iota((rows, LANES), 1) // 32


def send_kernel(drift, warm, near, send, out0, out1, out2, out3):
    outs = (out0, out1, out2, out3)
    width, fibres = drift.shape
    quarter = width // 4
    warm_now = warm[...]
    velocity = split(drift[...] + warm_now, 3)
    slots = iota((fibres, LANES), 0)
    leaving = join(dot(split(warm_now, 3), onehot(slots == row_of(send[...]))), 3)
    group = lane_group(quarter)
    for pair in range(2):
        hot = jnp.concatenate([onehot(slots == near[2 * pair + i:2 * pair + i + 1, :]) for i in range(2)], axis=1)
        picked = join(dot(velocity, hot), 3)
        for i in range(2):
            face = 2 * pair + i
            packed = jnp.zeros((quarter, LANES), F32)
            for q in range(4):
                rows = leaving[q * quarter:(q + 1) * quarter]
                moved = pltpu.roll(rows, (32 * (q - face)) % LANES, 1) if q != face else rows
                packed = jnp.where(group == q, moved, packed)
            outs[face][:width, :] = picked[:, i * LANES:(i + 1) * LANES]
            outs[face][width:, :] = packed


def setup_kernel(live, drift, warm, gap, near, send, land, contacts,
                 table, hot_first, hot_near, partial, lam, near_state):
    width, fibres = drift.shape
    count = contacts.shape[1]
    total = table.shape[0]
    halo = total - fibres - LANES
    near_all = halo

    land_row = row_of(land[...])
    land_column = column(land_row)

    def build(n, _):
        at = pl.ds(pl.multiple_of(n * CHUNK, CHUNK), CHUNK)
        alive = n * CHUNK + iota((1, CHUNK), 1) < live[0]
        first = jnp.where(alive, contacts[0:1, at], -1)
        second = jnp.where(alive, contacts[1:2, at], -1)
        for start in range(0, total - LANES, 256):
            ids = start + iota((256, CHUNK), 0)
            table[start:start + 256, at] = jnp.where(
                ids == first, 1.0, jnp.where(ids == second, -1.0, 0.0)).astype(BF16)
        table[total - LANES:, at] = jnp.where(
            land_column == first, 1.0, jnp.where(land_column == second, -1.0, 0.0)).astype(BF16)
        return 0

    lax.fori_loop(0, count // CHUNK, build, 0)

    def build_first(n, _):
        at = pl.ds(pl.multiple_of(n * LANES, LANES), LANES)
        first = column(contacts[0:1, at])
        hot_first[at, :] = onehot(first == iota((LANES, fibres), 1))
        for face in range(4):
            hot_near[at, face * LANES:(face + 1) * LANES] = onehot(first == near[face:face + 1, :])
        return 0

    lax.fori_loop(0, count // LANES, build_first, 0)

    slots = iota((LANES, fibres), 0)
    taken = (column(row_of(send[...])) == iota((LANES, fibres), 1)) | (land_column == iota((LANES, fibres), 1))
    keep = jnp.max(jnp.where(taken, 1.0, 0.0), axis=0, keepdims=True) < 0.5
    lam_now = jnp.where(keep, warm[...], 0.0)
    lam[...] = lam_now

    slots = iota((fibres, LANES), 0)
    for pair in range(2):
        hot = jnp.concatenate([onehot(slots == near[2 * pair + i:2 * pair + i + 1, :]) for i in range(2)], axis=1)
        at = slice(pair * 256, pair * 256 + 256)
        near_state[0, :, at] = join(dot(split(drift[...], 3), hot), 3)
        near_state[1, :, at] = join(dot(split(gap[...], 3), hot), 3)
        near_state[2, :, at] = join(dot(split(warm[...], 3), hot), 3)

    own_part(drift, lam, table, partial)


def own_part(drift, lam, table, partial):
    fibres = drift.shape[1]
    velocity = split(drift[...] + lam[...], 3)

    def body(n, _):
        at = pl.ds(pl.multiple_of(n * CHUNK, CHUNK), CHUNK)
        partial[:, at] = join(dot(velocity, table[:fibres, at]), 3)
        return 0

    lax.fori_loop(0, partial.shape[1] // CHUNK, body, 0)


def halo_blocks(ends, parts, width):
    below = jnp.where(ends[0] == 0, 0.0, parts[0][:width, :])
    above = jnp.where(ends[1] == 0, 0.0, parts[1][:width, :])
    return [below, above, parts[2][:width, :], parts[3][:width, :]]


def rate_body(partial, extra, table, base, stacked, contacts, rate_out):
    width, count = partial.shape
    kinds = stacked.shape[0] // width
    rows = extra.shape[1]

    def body(n, _):
        at = pl.ds(pl.multiple_of(n * CHUNK, CHUNK), CHUNK)
        far = join(dot(extra, table[base:base + rows, at]), 3)
        diff = (partial[:, at] + far).astype(BF16)
        kind = contacts[2:3, at]
        full = dot(stacked[...], diff)
        rate = full[:width]
        for i in range(1, kinds):
            rate = jnp.where(kind == i, full[i * width:(i + 1) * width], rate)
        rate_out[:, at] = split(rate, 2)
        return 0

    lax.fori_loop(0, count // CHUNK, body, 0)


def near_update(near_state, near_out, rate, hot_near, outs):
    for pair in range(2):
        at = slice(pair * 256, pair * 256 + 256)
        rates = join(dot(rate[...], hot_near[:, at]), 2)
        lam = project(near_state[2, :, at] - OMEGA * (rates + near_state[1, :, at]))
        near_out[:, at] = lam
        velocity = near_state[0, :, at] + lam
        for i in range(2):
            outs[2 * pair + i][...] = velocity[:, i * LANES:(i + 1) * LANES]


def first_kernel(ends, below, above, left, right, land, lam_in, partial, table, stacked, contacts,
                 hot_near, near_state, rate, near_lam, lam, out0, out1, out2, out3):
    width, fibres = lam_in.shape
    quarter = width // 4
    parts = (below, above, left, right)
    group = lane_group(quarter)
    arrived = []
    for q in range(4):
        block = jnp.zeros((quarter, LANES), F32)
        for face in range(4):
            rows = parts[face][width:, :]
            if face < 2:
                rows = jnp.where(ends[face] == 0, 0.0, rows)
            moved = pltpu.roll(rows, (32 * (face - q)) % LANES, 1) if q != face else rows
            block = jnp.where(group == face, moved, block)
        arrived.append(block)
    arrived = jnp.concatenate(arrived, axis=0)
    extra = split(jnp.concatenate(halo_blocks(ends, parts, width) + [arrived], axis=1), 3)
    rate_body(partial, extra, table, fibres, stacked, contacts, rate)
    near_update(near_state, near_lam, rate, hot_near, (out0, out1, out2, out3))
    hot = onehot(column(row_of(land[...])) == iota((LANES, fibres), 1))
    lam[...] = lam_in[...] + join(dot(split(arrived, 3), hot), 3)


def sweep_kernel(ends, below, above, left, right, partial, table, stacked, contacts,
                 hot_near, near_state, near_in, rate, near_lam, out0, out1, out2, out3):
    width = partial.shape[0]
    parts = (below, above, left, right)
    extra = split(jnp.concatenate(halo_blocks(ends, parts, width), axis=1), 3)
    fibres = table.shape[0] - LANES - extra.shape[1]
    rate_body(partial, extra, table, fibres, stacked, contacts, rate)
    outs = (out0, out1, out2, out3)
    for pair in range(2):
        at = slice(pair * 256, pair * 256 + 256)
        rates = join(dot(rate[...], hot_near[:, at]), 2)
        lam = project(near_in[:, at] - OMEGA * (rates + near_state[1, :, at]))
        near_lam[:, at] = lam
        velocity = near_state[0, :, at] + lam
        for i in range(2):
            outs[2 * pair + i][...] = velocity[:, i * LANES:(i + 1) * LANES]


def update(rate, hot_first, lam_in, gap, lam, rates=None):
    fibres = lam_in.shape[1]
    for start in range(0, fibres, CHUNK):
        at = slice(start, start + CHUNK)
        total = join(dot(rate[...], hot_first[:, at]), 2)
        lam[:, at] = project(lam_in[:, at] - OMEGA * (total + gap[:, at]))
        if rates is not None:
            rates[:, at] = total


def own_kernel(rate, hot_first, lam_in, gap, drift, table, lam, partial):
    update(rate, hot_first, lam_in, gap, lam)
    own_part(drift, lam, table, partial)


def last_kernel(ends, below, above, left, right, partial, table, stacked, contacts,
                hot_first, lam_in, gap, lam, rates, rate):
    width = partial.shape[0]
    parts = (below, above, left, right)
    extra = split(jnp.concatenate(halo_blocks(ends, parts, width), axis=1), 3)
    fibres = table.shape[0] - LANES - extra.shape[1]
    rate_body(partial, extra, table, fibres, stacked, contacts, rate)
    update(rate, hot_first, lam_in, gap, lam, rates)


def call(kernel, outs, args, scalars=0, scratch=(), flops=0):
    whole = pl.BlockSpec(memory_space=pltpu.VMEM)
    scalar = pl.BlockSpec(memory_space=pltpu.SMEM)
    return pl.pallas_call(
        kernel,
        out_shape=[jax.ShapeDtypeStruct(s, d) for s, d in outs],
        in_specs=[scalar] * scalars + [whole] * (len(args) - scalars),
        out_specs=[whole] * len(outs),
        scratch_shapes=list(scratch),
        compiler_params=pltpu.CompilerParams(vmem_limit_bytes=VMEM_LIMIT),
        cost_estimate=pl.CostEstimate(flops=flops, bytes_accessed=4 << 20, transcendentals=0),
    )(*args)


def per_device(drift, warm, gap, mobility, near_list, send_slot, land_slot, contacts, live):
    width, fibres = drift.shape[0] * drift.shape[1], drift.shape[2]
    count = contacts.shape[1]
    near = near_list.shape[0] * near_list.shape[1]
    shape = drift.shape
    drift, warm, gap = (x.reshape(width, fibres) for x in (drift, warm, gap))
    stacked = mobility.reshape(-1, width)
    place = lax.axis_index("grav")
    ends = jnp.stack([place > 0, place < lax.axis_size("grav") - 1]).astype(jnp.int32)

    total = fibres + near + LANES
    face = ((width, LANES), F32)
    big = ((width, fibres), F32)
    rate_shape = ((2 * width, count), BF16)
    near_shape = ((width, near), F32)
    partial_shape = ((width, count), F32)

    sent = call(send_kernel, [((width + width // 4, LANES), F32)] * 4, (drift, warm, near_list, send_slot),
                flops=2 << 30)
    halo = exchange(sent)
    table, hot_first, hot_near, partial, lam, near_state = call(
        setup_kernel,
        [((total, count), BF16), ((count, fibres), BF16), ((count, near), BF16), partial_shape, big,
         ((3, width, near), F32)],
        (live, drift, warm, gap, near_list, send_slot, land_slot, contacts), scalars=1, flops=8 << 30)
    rate, near_lam, lam, *sent = call(
        first_kernel, [rate_shape, near_shape, big] + [face] * 4,
        (ends, *halo, land_slot, lam, partial, table, stacked, contacts, hot_near, near_state), scalars=1,
        flops=4 << 30)
    for repeat in range(1, SWEEPS):
        halo = exchange(sent)
        lam, partial = call(own_kernel, [big, partial_shape], (rate, hot_first, lam, gap, drift, table),
                            flops=8 << 30)
        if repeat < SWEEPS - 1:
            rate, near_lam, *sent = call(
                sweep_kernel, [rate_shape, near_shape] + [face] * 4,
                (ends, *halo, partial, table, stacked, contacts, hot_near, near_state, near_lam), scalars=1,
                flops=4 << 30)
    lam, rates = call(
        last_kernel, [big, big],
        (ends, *halo, partial, table, stacked, contacts, hot_first, lam, gap), scalars=1,
        scratch=[pltpu.VMEM(*rate_shape)], flops=4 << 30)
    return lam.reshape(shape), rates.reshape(shape)


def solution(mesh):
    both = ("grav", "cross")
    return jax.shard_map(
        per_device,
        mesh=mesh,
        in_specs=(
            P(None, None, both),
            P(None, None, both),
            P(None, None, both),
            P(),
            P(None, both),
            P(None, both),
            P(None, both),
            P(None, both),
            P(both),
        ),
        out_specs=(P(None, None, both), P(None, None, both)),
        check_vma=False,
    )
```

```python
import functools

import jax
import jax.numpy as jnp
from jax import lax
from jax.experimental import pallas as pl
from jax.experimental.pallas import tpu as pltpu
from jax.sharding import PartitionSpec as P

SWEEPS = 3
OMEGA = 0.5
FRICTION = 0.4
LANES = 128
CHUNK = 256
VMEM_LIMIT = 24 * 1024 * 1024
F32 = jnp.float32
BF16 = jnp.bfloat16


def swap(x, axis, offset):
    count = lax.axis_size(axis)
    pairs = []
    for low in range(offset, count, 2):
        high = (low + 1) % count
        if axis == "grav" and high < low:
            pairs += [(low, low), (high, high)]
        else:
            pairs += [(low, high), (high, low)]
    return lax.ppermute(x, axis, pairs)


def exchange(sent):
    return (swap(sent[0], "cross", 1), swap(sent[1], "cross", 0), swap(sent[2], "grav", 0), swap(sent[3], "grav", 1))


def odd(axis):
    return lax.rem(lax.axis_index(axis), 2) == 1


def outgoing(faces):
    c, g = odd("cross"), odd("grav")
    return (jnp.where(c, faces[3], faces[2]), jnp.where(c, faces[2], faces[3]),
            jnp.where(g, faces[0], faces[1]), jnp.where(g, faces[1], faces[0]))


def incoming(parts):
    c, g = odd("cross"), odd("grav")
    place = lax.axis_index("grav")
    below, above = jnp.where(g, parts[2], parts[3]), jnp.where(g, parts[3], parts[2])
    return [jnp.where(place == 0, 0.0, below), jnp.where(place == lax.axis_size("grav") - 1, 0.0, above),
            jnp.where(c, parts[1], parts[0]), jnp.where(c, parts[0], parts[1])]


def split(x, parts):
    out = []
    for _ in range(parts - 1):
        part = x.astype(BF16)
        out.append(part)
        x = x - part.astype(F32)
    out.append(x.astype(BF16))
    return jnp.concatenate(out, axis=0)


def join(y, parts):
    rows = y.shape[0] // parts
    total = y[(parts - 1) * rows:]
    for i in range(parts - 2, -1, -1):
        total = total + y[i * rows:(i + 1) * rows]
    return total


def dot(a, b):
    return jnp.dot(a, b, preferred_element_type=F32)


def iota(shape, dim):
    return lax.broadcasted_iota(jnp.int32, shape, dim)


def narrow(x, shape):
    return jnp.broadcast_to(x, shape).astype(jnp.int16)


def onehot(ids, wanted):
    shape = jnp.broadcast_shapes(ids.shape, wanted.shape)
    one, zero = jnp.ones(shape, BF16), jnp.zeros(shape, BF16)
    return jnp.where(narrow(ids, shape) == narrow(wanted, shape), one, zero)


def signed(ids, first, second):
    shape = jnp.broadcast_shapes(ids.shape, first.shape)
    one, zero = jnp.ones(shape, BF16), jnp.zeros(shape, BF16)
    ids = narrow(ids, shape)
    return jnp.where(ids == narrow(first, shape), one, jnp.where(ids == narrow(second, shape), -one, zero))


def column(row):
    size = row.shape[1]
    eye = iota((size, size), 0) == iota((size, size), 1)
    return jnp.sum(jnp.where(eye, row.astype(F32), 0.0), axis=1, keepdims=True).astype(jnp.int32)


def row_of(table):
    return jnp.concatenate([table[i:i + 1] for i in range(table.shape[0])], axis=1)


def project(trial):
    third = trial.shape[0] // 3
    normal = jnp.maximum(trial[:third], 0.0)
    bound = FRICTION * normal
    first = jnp.minimum(jnp.maximum(trial[third:2 * third], -bound), bound)
    second = jnp.minimum(jnp.maximum(trial[2 * third:], -bound), bound)
    return jnp.concatenate([normal, first, second], axis=0)


def lane_group(rows):
    return iota((rows, LANES), 1) // 32


def send_kernel(drift_hbm, warm_hbm, near_hbm, send_hbm, out0, out1, out2, out3, velocity_out,
                drift, warm, near, send, sems):
    copies = [pltpu.make_async_copy(source, target, sems.at[i]) for i, (source, target) in enumerate(
        ((near_hbm, near), (send_hbm, send), (warm_hbm, warm), (drift_hbm, drift)))]
    for copy in copies:
        copy.start()
    for copy in copies:
        copy.wait()
    width, fibres = drift.shape
    quarter = width // 4
    warm_now = warm[...]
    velocity = split(drift[...] + warm_now, 3)
    slots = iota((fibres, LANES), 0)
    leaving = join(dot(split(warm_now, 3), onehot(slots, row_of(send[...]))), 3)
    group = lane_group(quarter)
    blocks = []
    for pair in range(2):
        hot = jnp.concatenate([onehot(slots, near[2 * pair + i:2 * pair + i + 1, :]) for i in range(2)], axis=1)
        picked = join(dot(velocity, hot), 3)
        velocity_out[:, pair * 256:pair * 256 + 256] = picked
        for i in range(2):
            face = 2 * pair + i
            packed = jnp.zeros((quarter, LANES), F32)
            for q in range(4):
                rows = leaving[q * quarter:(q + 1) * quarter]
                moved = pltpu.roll(rows, (32 * (q - face)) % LANES, 1) if q != face else rows
                packed = jnp.where(group == q, moved, packed)
            blocks.append((picked[:, i * LANES:(i + 1) * LANES], packed))
    for out, block, packed in zip((out0, out1, out2, out3), outgoing([b[0] for b in blocks]),
                                  outgoing([b[1] for b in blocks])):
        out[:width, :] = block
        out[width:, :] = packed


def setup_kernel(live, drift, warm, gap, near, send, land, contacts, mobility, near_velocity,
                 table, hot_first, hot_near, hot_land, kind, partial, lam, near_state, stacked):
    width, fibres = drift.shape
    count = contacts.shape[1]
    total = table.shape[0]

    land_row = row_of(land[...])
    land_column = column(land_row)

    for start in range(0, count, CHUNK):
        at = slice(start, start + CHUNK)
        alive = start + iota((1, CHUNK), 1) < live[0]
        first = jnp.where(alive, contacts[0:1, at], -1)
        second = jnp.where(alive, contacts[1:2, at], -1)
        for row in range(0, total - LANES, LANES):
            table[row:row + LANES, at] = signed(row + iota((LANES, CHUNK), 0), first, second)
        table[total - LANES:, at] = signed(land_column, first, second)

    for start in range(0, count, LANES):
        at = slice(start, start + LANES)
        first = column(contacts[0:1, at])
        hot_first[at, :] = onehot(first, iota((LANES, fibres), 1))
        for face in range(4):
            hot_near[at, face * LANES:(face + 1) * LANES] = onehot(first, near[face:face + 1, :])

    stacked[...] = jnp.concatenate([mobility[i] for i in range(mobility.shape[0])], axis=1)

    taken = (column(row_of(send[...])) == iota((LANES, fibres), 1)) | (land_column == iota((LANES, fibres), 1))
    keep = jnp.max(jnp.where(taken, 1.0, 0.0), axis=0, keepdims=True) < 0.5
    hot_land[...] = onehot(land_column, iota((LANES, fibres), 1))
    kind[...] = contacts[2:3, :]
    lam_now = jnp.where(keep, warm[...], 0.0)
    lam[...] = lam_now

    slots = iota((fibres, LANES), 0)
    for pair in range(2):
        hot = jnp.concatenate([onehot(slots, near[2 * pair + i:2 * pair + i + 1, :]) for i in range(2)], axis=1)
        at = slice(pair * 256, pair * 256 + 256)
        near_warm = join(dot(split(warm[...], 3), hot), 3)
        near_state[0, :, at] = near_velocity[:, at] - near_warm
        near_state[1, :, at] = join(dot(split(gap[...], 3), hot), 3)
        near_state[2, :, at] = near_warm

    own_part(drift, lam, table, partial)


def own_part(drift, lam, table, partial):
    fibres = drift.shape[1]
    velocity = split(drift[...] + lam[...], 3)

    for start in range(0, partial.shape[1], CHUNK):
        at = slice(start, start + CHUNK)
        partial[:, at] = join(dot(velocity, table[:fibres, at]), 3)


def rate_body(partial, extra, table, base, stacked, kind_row, rate_out):
    width, count = partial.shape
    kinds = stacked.shape[1] // width
    rows = extra.shape[1]
    for start in range(0, count, CHUNK):
        at = slice(start, start + CHUNK)
        far = join(dot(extra, table[base:base + rows, at]), 3)
        diff = (partial[:, at] + far).astype(BF16)
        kind = kind_row[:, at]
        none = jnp.zeros_like(diff)
        chosen = jnp.concatenate([jnp.where(kind == i, diff, none) for i in range(kinds)], axis=0)
        rate_out[:, at] = split(dot(stacked[...], chosen), 2)


def near_update(near_in, near_state, near_lam, rate, hot_near, outs):
    faces = []
    for pair in range(2):
        at = slice(pair * 256, pair * 256 + 256)
        rates = join(dot(rate[...], hot_near[:, at]), 2)
        lam = project(near_in[:, at] - OMEGA * (rates + near_state[1, :, at]))
        near_lam[:, at] = lam
        velocity = near_state[0, :, at] + lam
        faces += [velocity[:, i * LANES:(i + 1) * LANES] for i in range(2)]
    for out, block in zip(outs, outgoing(faces)):
        out[...] = block


def first_kernel(part0, part1, part2, part3, hot_land, lam_in, partial, table, stacked, kind,
                 hot_near, near_state, rate, near_lam, lam, out0, out1, out2, out3):
    width, fibres = lam_in.shape
    quarter = width // 4
    parts = (part0, part1, part2, part3)
    blocks = incoming([part[:width, :] for part in parts])
    packed = incoming([part[width:, :] for part in parts])
    group = lane_group(quarter)
    arrived = []
    for q in range(4):
        block = jnp.zeros((quarter, LANES), F32)
        for face in range(4):
            rows = packed[face]
            moved = pltpu.roll(rows, (32 * (face - q)) % LANES, 1) if q != face else rows
            block = jnp.where(group == face, moved, block)
        arrived.append(block)
    arrived = jnp.concatenate(arrived, axis=0)
    extra = split(jnp.concatenate(blocks + [arrived], axis=1), 3)
    rate_body(partial, extra, table, fibres, stacked, kind, rate)
    near_update(near_state[2], near_state, near_lam, rate, hot_near, (out0, out1, out2, out3))
    lam[...] = lam_in[...] + join(dot(split(arrived, 3), hot_land[...]), 3)


def sweep_kernel(part0, part1, part2, part3, partial, table, stacked, kind,
                 hot_near, near_state, near_in, rate, near_lam, out0, out1, out2, out3):
    parts = [part[...] for part in (part0, part1, part2, part3)]
    extra = split(jnp.concatenate(incoming(parts), axis=1), 3)
    fibres = table.shape[0] - LANES - extra.shape[1]
    rate_body(partial, extra, table, fibres, stacked, kind, rate)
    near_update(near_in, near_state, near_lam, rate, hot_near, (out0, out1, out2, out3))


def update(rate, hot_first, lam_in, gap, lam, rates=None):
    fibres = lam_in.shape[1]
    for start in range(0, fibres, CHUNK):
        at = slice(start, start + CHUNK)
        total = join(dot(rate[...], hot_first[:, at]), 2)
        lam[:, at] = project(lam_in[:, at] - OMEGA * (total + gap[:, at]))
        if rates is not None:
            rates[:, at] = total


def own_kernel(rate, hot_first, lam_in, gap, drift, table, lam, partial):
    update(rate, hot_first, lam_in, gap, lam)
    own_part(drift, lam, table, partial)


def last_kernel(part0, part1, part2, part3, partial, table, stacked, kind,
                hot_first, lam_in, gap, lam, rates, rate):
    parts = [part[...] for part in (part0, part1, part2, part3)]
    extra = split(jnp.concatenate(incoming(parts), axis=1), 3)
    fibres = table.shape[0] - LANES - extra.shape[1]
    rate_body(partial, extra, table, fibres, stacked, kind, rate)
    update(rate, hot_first, lam_in, gap, lam, rates)


def call(kernel, outs, args, scalars=0, scratch=(), flops=0, space=pltpu.VMEM):
    whole = pl.BlockSpec(memory_space=pltpu.VMEM)
    scalar = pl.BlockSpec(memory_space=pltpu.SMEM)
    return pl.pallas_call(
        kernel,
        out_shape=[jax.ShapeDtypeStruct(s, d) for s, d in outs],
        in_specs=[scalar] * scalars + [pl.BlockSpec(memory_space=space)] * (len(args) - scalars),
        out_specs=[whole] * len(outs),
        scratch_shapes=list(scratch),
        compiler_params=pltpu.CompilerParams(vmem_limit_bytes=VMEM_LIMIT),
        cost_estimate=pl.CostEstimate(flops=flops, bytes_accessed=4 << 20, transcendentals=0),
    )(*args)


def per_device(drift, warm, gap, mobility, near_list, send_slot, land_slot, contacts, live):
    width, fibres = drift.shape[0] * drift.shape[1], drift.shape[2]
    count = contacts.shape[1]
    near = near_list.shape[0] * near_list.shape[1]
    shape = drift.shape
    drift, warm, gap = (x.reshape(width, fibres) for x in (drift, warm, gap))
    total = fibres + near + LANES
    face = ((width, LANES), F32)
    big = ((width, fibres), F32)
    rate_shape = ((2 * width, count), BF16)
    near_shape = ((width, near), F32)
    partial_shape = ((width, count), F32)

    held = [pltpu.with_memory_space_constraint(x, pltpu.HBM) for x in (drift, warm, near_list, send_slot)]
    *sent, near_velocity = call(
        send_kernel, [((width + width // 4, LANES), F32)] * 4 + [near_shape], held, flops=2 << 30, space=pltpu.HBM,
        scratch=[pltpu.VMEM(x.shape, x.dtype) for x in held] + [pltpu.SemaphoreType.DMA((len(held),))])
    halo = exchange(sent)
    table, hot_first, hot_near, hot_land, kind, partial, lam, near_state, stacked = call(
        setup_kernel,
        [((total, count), BF16), ((count, fibres), BF16), ((count, near), BF16), ((LANES, fibres), BF16),
         ((1, count), jnp.int32), partial_shape, big, ((3, width, near), F32),
         ((width, mobility.shape[0] * width), BF16)],
        (live, drift, warm, gap, near_list, send_slot, land_slot, contacts, mobility, near_velocity), scalars=1,
        flops=8 << 30)
    rate, near_lam, lam, *sent = call(
        first_kernel, [rate_shape, near_shape, big] + [face] * 4,
        (*halo, hot_land, lam, partial, table, stacked, kind, hot_near, near_state),
        flops=4 << 30)
    for repeat in range(1, SWEEPS):
        halo = exchange(sent)
        lam, partial = call(own_kernel, [big, partial_shape], (rate, hot_first, lam, gap, drift, table),
                            flops=8 << 30)
        if repeat < SWEEPS - 1:
            rate, near_lam, *sent = call(
                sweep_kernel, [rate_shape, near_shape] + [face] * 4,
                (*halo, partial, table, stacked, kind, hot_near, near_state, near_lam),
                flops=4 << 30)
    lam, rates = call(
        last_kernel, [big, big],
        (*halo, partial, table, stacked, kind, hot_first, lam, gap),
        scratch=[pltpu.VMEM(*rate_shape)], flops=4 << 30)
    return lam.reshape(shape), rates.reshape(shape)


def solution(mesh):
    both = ("grav", "cross")
    return jax.shard_map(
        per_device,
        mesh=mesh,
        in_specs=(
            P(None, None, both),
            P(None, None, both),
            P(None, None, both),
            P(),
            P(None, both),
            P(None, both),
            P(None, both),
            P(None, both),
            P(both),
        ),
        out_specs=(P(None, None, both), P(None, None, both)),
        check_vma=False,
    )
```

```python
import functools

import jax
import jax.numpy as jnp
from jax import lax
from jax.experimental import pallas as pl
from jax.experimental.pallas import tpu as pltpu
from jax.sharding import PartitionSpec as P

SWEEPS = 3
OMEGA = 0.5
FRICTION = 0.4
LANES = 128
CHUNK = 256
RATE_SIZE = 1024
VMEM_LIMIT = 24 * 1024 * 1024
F32 = jnp.float32
BF16 = jnp.bfloat16


def swap(x, axis, offset):
    count = lax.axis_size(axis)
    pairs = []
    for low in range(offset, count, 2):
        high = (low + 1) % count
        if axis == "grav" and high < low:
            pairs += [(low, low), (high, high)]
        else:
            pairs += [(low, high), (high, low)]
    return lax.ppermute(x, axis, pairs)


def exchange(sent):
    steps = (("cross", 1), ("cross", 0), ("grav", 0), ("grav", 1))
    return [swap(block, *step) for block, step in zip(sent, steps)]


def odd(axis):
    return lax.rem(lax.axis_index(axis), 2) == 1


def outgoing(faces):
    c, g = odd("cross"), odd("grav")
    steps = (jnp.where(c, faces[3], faces[2]), jnp.where(c, faces[2], faces[3]),
             jnp.where(g, faces[0], faces[1]), jnp.where(g, faces[1], faces[0]))
    return steps


def incoming(parts):
    c, g = odd("cross"), odd("grav")
    place = lax.axis_index("grav")
    below, above = jnp.where(g, parts[2], parts[3]), jnp.where(g, parts[3], parts[2])
    return [jnp.where(place == 0, 0.0, below), jnp.where(place == lax.axis_size("grav") - 1, 0.0, above),
            jnp.where(c, parts[1], parts[0]), jnp.where(c, parts[0], parts[1])]


def split(x, parts):
    out = []
    for _ in range(parts - 1):
        part = x.astype(BF16)
        out.append(part)
        x = x - part.astype(F32)
    out.append(x.astype(BF16))
    return jnp.concatenate(out, axis=0)


def join(y, parts):
    rows = y.shape[0] // parts
    total = y[(parts - 1) * rows:]
    for i in range(parts - 2, -1, -1):
        total = total + y[i * rows:(i + 1) * rows]
    return total


def dot(a, b):
    return jnp.dot(a, b, preferred_element_type=F32)


def iota(shape, dim):
    return lax.broadcasted_iota(jnp.int32, shape, dim)


def narrow(x, shape):
    return jnp.broadcast_to(x, shape).astype(jnp.int16)


def onehot(ids, wanted):
    shape = jnp.broadcast_shapes(ids.shape, wanted.shape)
    one, zero = jnp.ones(shape, BF16), jnp.zeros(shape, BF16)
    return jnp.where(narrow(ids, shape) == narrow(wanted, shape), one, zero)


def signed(ids, first, second):
    shape = jnp.broadcast_shapes(ids.shape, first.shape)
    one, zero = jnp.ones(shape, BF16), jnp.zeros(shape, BF16)
    ids = narrow(ids, shape)
    return jnp.where(ids == narrow(first, shape), one, jnp.where(ids == narrow(second, shape), -one, zero))


def column(row):
    size = row.shape[1]
    eye = iota((size, size), 0) == iota((size, size), 1)
    return jnp.sum(jnp.where(eye, row.astype(F32), 0.0), axis=1, keepdims=True).astype(jnp.int32)


def row_of(table):
    return jnp.concatenate([table[i:i + 1] for i in range(table.shape[0])], axis=1)


def project(trial):
    third = trial.shape[0] // 3
    normal = jnp.maximum(trial[:third], 0.0)
    bound = FRICTION * normal
    first = jnp.minimum(jnp.maximum(trial[third:2 * third], -bound), bound)
    second = jnp.minimum(jnp.maximum(trial[2 * third:], -bound), bound)
    return jnp.concatenate([normal, first, second], axis=0)


def lane_group(rows):
    return iota((rows, LANES), 1) // 32


def send_kernel(drift_hbm, warm_hbm, near_hbm, send_hbm, out0, out1, out2, out3, velocity_out,
                drift, warm, near, send, sems, hot_near, hot_send):
    copies = [pltpu.make_async_copy(source, target, sems.at[i]) for i, (source, target) in enumerate(
        ((near_hbm, near), (send_hbm, send), (warm_hbm, warm), (drift_hbm, drift)))]
    for copy in copies:
        copy.start()
    width, fibres = drift.shape
    quarter = width // 4
    slots = iota((fibres, LANES), 0)
    copies[0].wait()
    for face in range(4):
        hot_near[:, face * LANES:(face + 1) * LANES] = onehot(slots, near[face:face + 1, :])
    copies[1].wait()
    hot_send[...] = onehot(slots, row_of(send[...]))
    copies[2].wait()
    warm_now = warm[...]
    leaving = join(dot(split(warm_now, 3), hot_send[...]), 3)
    copies[3].wait()
    velocity = split(drift[...] + warm_now, 3)
    group = lane_group(quarter)
    blocks = []
    for pair in range(2):
        picked = join(dot(velocity, hot_near[:, pair * 256:pair * 256 + 256]), 3)
        velocity_out[:, pair * 256:pair * 256 + 256] = picked
        for i in range(2):
            face = 2 * pair + i
            packed = jnp.zeros((quarter, LANES), F32)
            for q in range(4):
                rows = leaving[q * quarter:(q + 1) * quarter]
                moved = pltpu.roll(rows, (32 * (q - face)) % LANES, 1) if q != face else rows
                packed = jnp.where(group == q, moved, packed)
            blocks.append((picked[:, i * LANES:(i + 1) * LANES], packed))
    for out, block, packed in zip((out0, out1, out2, out3), outgoing([b[0] for b in blocks]),
                                  outgoing([b[1] for b in blocks])):
        out[:width, :] = block
        out[width:, :] = packed


def setup_kernel(live, drift, warm, gap, near, send, land, contacts, mobility, near_velocity,
                 table, hot_first, hot_near, hot_land, kind, partial, lam, near_state, stacked):
    width, fibres = drift.shape
    count = contacts.shape[1]
    total = table.shape[0]

    land_row = row_of(land[...])
    land_column = column(land_row)

    for start in range(0, count, CHUNK):
        at = slice(start, start + CHUNK)
        alive = start + iota((1, CHUNK), 1) < live[0]
        first = jnp.where(alive, contacts[0:1, at], -1)
        second = jnp.where(alive, contacts[1:2, at], -1)
        for row in range(0, total - LANES, LANES):
            table[row:row + LANES, at] = signed(row + iota((LANES, CHUNK), 0), first, second)
        table[total - LANES:, at] = signed(land_column, first, second)

    for start in range(0, count, LANES):
        at = slice(start, start + LANES)
        first = column(contacts[0:1, at])
        hot_first[at, :] = onehot(first, iota((LANES, fibres), 1))
        for face in range(4):
            hot_near[at, face * LANES:(face + 1) * LANES] = onehot(first, near[face:face + 1, :])

    stacked[...] = jnp.concatenate([mobility[i] for i in range(mobility.shape[0])], axis=1)

    taken = (column(row_of(send[...])) == iota((LANES, fibres), 1)) | (land_column == iota((LANES, fibres), 1))
    keep = jnp.max(jnp.where(taken, 1.0, 0.0), axis=0, keepdims=True) < 0.5
    hot_land[...] = onehot(land_column, iota((LANES, fibres), 1))
    kind[...] = contacts[2:3, :]
    lam_now = jnp.where(keep, warm[...], 0.0)
    lam[...] = lam_now

    slots = iota((fibres, LANES), 0)
    for pair in range(2):
        hot = jnp.concatenate([onehot(slots, near[2 * pair + i:2 * pair + i + 1, :]) for i in range(2)], axis=1)
        at = slice(pair * 256, pair * 256 + 256)
        near_warm = join(dot(split(warm[...], 3), hot), 3)
        near_state[0, :, at] = near_velocity[:, at] - near_warm
        near_state[1, :, at] = join(dot(split(gap[...], 3), hot), 3)
        near_state[2, :, at] = near_warm

    own_part(drift, lam, table, partial)


def own_part(drift, lam, table, partial):
    fibres = drift.shape[1]
    velocity = split(drift[...] + lam[...], 3)

    for start in range(0, partial.shape[1], CHUNK):
        at = slice(start, start + CHUNK)
        partial[:, at] = join(dot(velocity, table[:fibres, at]), 3)


def rate_body(partial, extra, table, base, stacked, kind_row, rate_out):
    width, count = partial.shape
    kinds = stacked.shape[1] // width
    rows = extra.shape[1]
    for start in range(0, count, RATE_SIZE):
        at = slice(start, start + RATE_SIZE)
        far = join(dot(extra[...], table[base:base + rows, at]), 3)
        diff = (partial[:, at] + far).astype(BF16)
        kind = kind_row[:, at]
        none = jnp.zeros_like(diff)
        chosen = jnp.concatenate([jnp.where(kind == i, diff, none) for i in range(kinds)], axis=0)
        rate_out[:, at] = split(dot(stacked[...], chosen), 2)


def near_update(near_in, near_state, near_lam, rate, hot_near, outs):
    faces = []
    for pair in range(2):
        at = slice(pair * 256, pair * 256 + 256)
        rates = join(dot(rate[...], hot_near[:, at]), 2)
        lam = project(near_in[:, at] - OMEGA * (rates + near_state[1, :, at]))
        near_lam[:, at] = lam
        velocity = near_state[0, :, at] + lam
        faces += [velocity[:, i * LANES:(i + 1) * LANES] for i in range(2)]
    for out, block in zip(outs, outgoing(faces)):
        out[...] = block


def first_kernel(part0, part1, part2, part3, hot_land, lam_in, partial, table, stacked, kind,
                 hot_near, near_state, rate, near_lam, lam, out0, out1, out2, out3, extra):
    width, fibres = lam_in.shape
    quarter = width // 4
    parts = (part0, part1, part2, part3)
    blocks = incoming([part[:width, :] for part in parts])
    packed = incoming([part[width:, :] for part in parts])
    group = lane_group(quarter)
    arrived = []
    for q in range(4):
        block = jnp.zeros((quarter, LANES), F32)
        for face in range(4):
            rows = packed[face]
            moved = pltpu.roll(rows, (32 * (face - q)) % LANES, 1) if q != face else rows
            block = jnp.where(group == face, moved, block)
        arrived.append(block)
    arrived = jnp.concatenate(arrived, axis=0)
    near = len(blocks) * LANES
    for i, block in enumerate(blocks + [arrived]):
        extra[:, i * LANES:(i + 1) * LANES] = split(block, 3)
    rate_body(partial, extra, table, fibres, stacked, kind, rate)
    near_update(near_state[2], near_state, near_lam, rate, hot_near, (out0, out1, out2, out3))
    lam[...] = lam_in[...] + join(dot(extra[:, near:], hot_land[...]), 3)


def sweep_kernel(part0, part1, part2, part3, partial, table, stacked, kind,
                 hot_near, near_state, near_in, rate, near_lam, out0, out1, out2, out3, extra):
    parts = [part[...] for part in (part0, part1, part2, part3)]
    for i, block in enumerate(incoming(parts)):
        extra[:, i * LANES:(i + 1) * LANES] = split(block, 3)
    fibres = table.shape[0] - LANES - extra.shape[1]
    rate_body(partial, extra, table, fibres, stacked, kind, rate)
    near_update(near_in, near_state, near_lam, rate, hot_near, (out0, out1, out2, out3))


def update(rate, hot_first, lam_in, gap, lam, at, rates=None):
    total = join(dot(rate[...], hot_first[:, at]), 2)
    lam[:, at] = project(lam_in[:, at] - OMEGA * (total + gap[:, at]))
    if rates is not None:
        rates[:, at] = total


def own_kernel(rate, hot_first, lam_in, gap, drift, table, lam, partial):
    for start in range(0, lam.shape[1], CHUNK):
        update(rate, hot_first, lam_in, gap, lam, slice(start, start + CHUNK))
    own_part(drift, lam, table, partial)


def last_kernel(part0, part1, part2, part3, partial, table, stacked, kind,
                hot_first, lam_in, gap, lam_out, rates_out, rate, extra, lam, rates, sems):
    parts = [part[...] for part in (part0, part1, part2, part3)]
    for i, block in enumerate(incoming(parts)):
        extra[:, i * LANES:(i + 1) * LANES] = split(block, 3)
    fibres = table.shape[0] - LANES - extra.shape[1]
    rate_body(partial, extra, table, fibres, stacked, kind, rate)
    copies = []
    for n, start in enumerate(range(0, lam.shape[1], CHUNK)):
        at = slice(start, start + CHUNK)
        update(rate, hot_first, lam_in, gap, lam, at, rates)
        for i, (source, target) in enumerate(((lam, lam_out), (rates, rates_out))):
            copy = pltpu.make_async_copy(source.at[:, at], target.at[:, at], sems.at[n, i])
            copy.start()
            copies.append(copy)
    for copy in copies:
        copy.wait()


def call(kernel, outs, args, scalars=0, scratch=(), flops=0, space=pltpu.VMEM, out_space=pltpu.VMEM):
    scalar = pl.BlockSpec(memory_space=pltpu.SMEM)
    return pl.pallas_call(
        kernel,
        out_shape=[jax.ShapeDtypeStruct(s, d) for s, d in outs],
        in_specs=[scalar] * scalars + [pl.BlockSpec(memory_space=space)] * (len(args) - scalars),
        out_specs=[pl.BlockSpec(memory_space=out_space)] * len(outs),
        scratch_shapes=list(scratch),
        compiler_params=pltpu.CompilerParams(vmem_limit_bytes=VMEM_LIMIT),
        cost_estimate=pl.CostEstimate(flops=flops, bytes_accessed=4 << 20, transcendentals=0),
    )(*args)


def per_device(drift, warm, gap, mobility, near_list, send_slot, land_slot, contacts, live):
    width, fibres = drift.shape[0] * drift.shape[1], drift.shape[2]
    count = contacts.shape[1]
    near = near_list.shape[0] * near_list.shape[1]
    shape = drift.shape
    drift, warm, gap = (x.reshape(width, fibres) for x in (drift, warm, gap))
    total = fibres + near + LANES
    face = ((width, LANES), F32)
    big = ((width, fibres), F32)
    rate_shape = ((2 * width, count), BF16)
    near_shape = ((width, near), F32)
    partial_shape = ((width, count), F32)

    held = [pltpu.with_memory_space_constraint(x, pltpu.HBM) for x in (drift, warm, near_list, send_slot)]
    *sent, near_velocity = call(
        send_kernel, [((width + width // 4, LANES), F32)] * 4 + [near_shape], held, flops=2 << 30, space=pltpu.HBM,
        scratch=[pltpu.VMEM(x.shape, x.dtype) for x in held] + [pltpu.SemaphoreType.DMA((len(held),)), pltpu.VMEM((fibres, near), BF16), pltpu.VMEM((fibres, LANES), BF16)])
    halo = exchange(sent)
    table, hot_first, hot_near, hot_land, kind, partial, lam, near_state, stacked = call(
        setup_kernel,
        [((total, count), BF16), ((count, fibres), BF16), ((count, near), BF16), ((LANES, fibres), BF16),
         ((1, count), jnp.int32), partial_shape, big, ((3, width, near), F32),
         ((width, mobility.shape[0] * width), BF16)],
        (live, drift, warm, gap, near_list, send_slot, land_slot, contacts, mobility, near_velocity), scalars=1,
        flops=8 << 30)
    rate, near_lam, lam, *sent = call(
        first_kernel, [rate_shape, near_shape, big] + [face] * 4,
        (*halo, hot_land, lam, partial, table, stacked, kind, hot_near, near_state),
        scratch=[pltpu.VMEM((3 * width, near + LANES), BF16)], flops=4 << 30)
    for repeat in range(1, SWEEPS):
        halo = exchange(sent)
        lam, partial = call(own_kernel, [big, partial_shape], (rate, hot_first, lam, gap, drift, table),
                            flops=8 << 30)
        extra = pltpu.VMEM((3 * width, near), BF16)
        if repeat < SWEEPS - 1:
            rate, near_lam, *sent = call(
                sweep_kernel, [rate_shape, near_shape] + [face] * 4,
                (*halo, partial, table, stacked, kind, hot_near, near_state, near_lam),
                scratch=[extra], flops=4 << 30)
    lam, rates = call(
        last_kernel, [big, big],
        (*halo, partial, table, stacked, kind, hot_first, lam, gap),
        scratch=[pltpu.VMEM(*rate_shape), extra, pltpu.VMEM(*big), pltpu.VMEM(*big),
                 pltpu.SemaphoreType.DMA((fibres // CHUNK, 2))], flops=4 << 30, out_space=pltpu.HBM)
    return lam.reshape(shape), rates.reshape(shape)


def solution(mesh):
    both = ("grav", "cross")
    return jax.shard_map(
        per_device,
        mesh=mesh,
        in_specs=(
            P(None, None, both),
            P(None, None, both),
            P(None, None, both),
            P(),
            P(None, both),
            P(None, both),
            P(None, both),
            P(None, both),
            P(both),
        ),
        out_specs=(P(None, None, both), P(None, None, both)),
        check_vma=False,
    )
```

```python
import functools

import jax
import jax.numpy as jnp
from jax import lax
from jax.experimental import pallas as pl
from jax.experimental.pallas import tpu as pltpu
from jax.sharding import PartitionSpec as P

SWEEPS = 3
OMEGA = 0.5
FRICTION = 0.4
LANES = 128
CHUNK = 256
RATE_SIZE = 1024
VMEM_LIMIT = 24 * 1024 * 1024
F32 = jnp.float32
BF16 = jnp.bfloat16


def swap(x, axis, offset):
    count = lax.axis_size(axis)
    pairs = []
    for low in range(offset, count, 2):
        high = (low + 1) % count
        pairs += [(low, high), (high, low)]
    return lax.ppermute(x, axis, pairs)


def exchange(sent):
    steps = (("cross", 1), ("cross", 0), ("grav", 0), ("grav", 1))
    return [swap(block, *step) for block, step in zip(sent, steps)]


def odd(axis):
    return lax.rem(lax.axis_index(axis), 2) == 1


def outgoing(faces):
    c, g = odd("cross"), odd("grav")
    steps = (jnp.where(c, faces[3], faces[2]), jnp.where(c, faces[2], faces[3]),
             jnp.where(g, faces[0], faces[1]), jnp.where(g, faces[1], faces[0]))
    return steps


def incoming(parts):
    c, g = odd("cross"), odd("grav")
    place = lax.axis_index("grav")
    below, above = jnp.where(g, parts[2], parts[3]), jnp.where(g, parts[3], parts[2])
    return [jnp.where(place == 0, 0.0, below), jnp.where(place == lax.axis_size("grav") - 1, 0.0, above),
            jnp.where(c, parts[1], parts[0]), jnp.where(c, parts[0], parts[1])]


def split(x, parts):
    out = []
    for _ in range(parts - 1):
        part = x.astype(BF16)
        out.append(part)
        x = x - part.astype(F32)
    out.append(x.astype(BF16))
    return jnp.concatenate(out, axis=0)


def join(y, parts):
    rows = y.shape[0] // parts
    total = y[(parts - 1) * rows:]
    for i in range(parts - 2, -1, -1):
        total = total + y[i * rows:(i + 1) * rows]
    return total


def dot(a, b):
    return jnp.dot(a, b, preferred_element_type=F32)


def iota(shape, dim):
    return lax.broadcasted_iota(jnp.int32, shape, dim)


def narrow(x, shape):
    return jnp.broadcast_to(x, shape).astype(jnp.int16)


def onehot(ids, wanted):
    shape = jnp.broadcast_shapes(ids.shape, wanted.shape)
    one, zero = jnp.ones(shape, BF16), jnp.zeros(shape, BF16)
    return jnp.where(narrow(ids, shape) == narrow(wanted, shape), one, zero)


def signed(ids, first, second):
    shape = jnp.broadcast_shapes(ids.shape, first.shape)
    one, zero = jnp.ones(shape, BF16), jnp.zeros(shape, BF16)
    ids = narrow(ids, shape)
    return jnp.where(ids == narrow(first, shape), one, jnp.where(ids == narrow(second, shape), -one, zero))


def column(row):
    size = row.shape[1]
    eye = iota((size, size), 0) == iota((size, size), 1)
    return jnp.sum(jnp.where(eye, row.astype(F32), 0.0), axis=1, keepdims=True).astype(jnp.int32)


def row_of(table):
    return jnp.concatenate([table[i:i + 1] for i in range(table.shape[0])], axis=1)


def project(trial):
    third = trial.shape[0] // 3
    normal = jnp.maximum(trial[:third], 0.0)
    bound = FRICTION * normal
    first = jnp.minimum(jnp.maximum(trial[third:2 * third], -bound), bound)
    second = jnp.minimum(jnp.maximum(trial[2 * third:], -bound), bound)
    return jnp.concatenate([normal, first, second], axis=0)


def lane_group(rows):
    return iota((rows, LANES), 1) // 32


def send_kernel(drift_hbm, warm_hbm, near_hbm, send_hbm, out0, out1, out2, out3, velocity_out,
                drift, warm, near, send, sems, hot_near, hot_send):
    copies = [pltpu.make_async_copy(source, target, sems.at[i]) for i, (source, target) in enumerate(
        ((near_hbm, near), (send_hbm, send), (warm_hbm, warm), (drift_hbm, drift)))]
    for copy in copies:
        copy.start()
    width, fibres = drift.shape
    quarter = width // 4
    slots = iota((fibres, LANES), 0)
    copies[0].wait()
    for face in range(4):
        hot_near[:, face * LANES:(face + 1) * LANES] = onehot(slots, near[face:face + 1, :])
    copies[1].wait()
    hot_send[...] = onehot(slots, row_of(send[...]))
    copies[2].wait()
    warm_now = warm[...]
    leaving = join(dot(split(warm_now, 3), hot_send[...]), 3)
    copies[3].wait()
    velocity = split(drift[...] + warm_now, 3)
    group = lane_group(quarter)
    blocks = []
    for pair in range(2):
        picked = join(dot(velocity, hot_near[:, pair * 256:pair * 256 + 256]), 3)
        velocity_out[:, pair * 256:pair * 256 + 256] = picked
        for i in range(2):
            face = 2 * pair + i
            packed = jnp.zeros((quarter, LANES), F32)
            for q in range(4):
                rows = leaving[q * quarter:(q + 1) * quarter]
                moved = pltpu.roll(rows, (32 * (q - face)) % LANES, 1) if q != face else rows
                packed = jnp.where(group == q, moved, packed)
            blocks.append((picked[:, i * LANES:(i + 1) * LANES], packed))
    for out, block, packed in zip((out0, out1, out2, out3), outgoing([b[0] for b in blocks]),
                                  outgoing([b[1] for b in blocks])):
        out[:width, :] = block
        out[width:, :] = packed


def setup_kernel(live, drift, warm, gap, near, send, land, contacts, mobility, near_velocity,
                 table, hot_first, hot_near, hot_land, kind, partial, lam, near_state, stacked):
    width, fibres = drift.shape
    count = contacts.shape[1]
    total = table.shape[0]

    land_row = row_of(land[...])
    land_column = column(land_row)

    for start in range(0, count, CHUNK):
        at = slice(start, start + CHUNK)
        alive = start + iota((1, CHUNK), 1) < live[0]
        first = jnp.where(alive, contacts[0:1, at], -1)
        second = jnp.where(alive, contacts[1:2, at], -1)
        for row in range(0, total - LANES, LANES):
            table[row:row + LANES, at] = signed(row + iota((LANES, CHUNK), 0), first, second)
        table[total - LANES:, at] = signed(land_column, first, second)

    for start in range(0, count, LANES):
        at = slice(start, start + LANES)
        first = column(contacts[0:1, at])
        hot_first[at, :] = onehot(first, iota((LANES, fibres), 1))
        for face in range(4):
            hot_near[at, face * LANES:(face + 1) * LANES] = onehot(first, near[face:face + 1, :])

    stacked[...] = jnp.concatenate([mobility[i] for i in range(mobility.shape[0])], axis=1)

    taken = (column(row_of(send[...])) == iota((LANES, fibres), 1)) | (land_column == iota((LANES, fibres), 1))
    keep = jnp.max(jnp.where(taken, 1.0, 0.0), axis=0, keepdims=True) < 0.5
    hot_land[...] = onehot(land_column, iota((LANES, fibres), 1))
    kind[...] = contacts[2:3, :]
    lam_now = jnp.where(keep, warm[...], 0.0)
    lam[...] = lam_now

    slots = iota((fibres, LANES), 0)
    for pair in range(2):
        hot = jnp.concatenate([onehot(slots, near[2 * pair + i:2 * pair + i + 1, :]) for i in range(2)], axis=1)
        at = slice(pair * 256, pair * 256 + 256)
        near_warm = join(dot(split(warm[...], 3), hot), 3)
        near_state[0, :, at] = near_velocity[:, at] - near_warm
        near_state[1, :, at] = join(dot(split(gap[...], 3), hot), 3)
        near_state[2, :, at] = near_warm

    own_part(drift, lam, table, partial)


def own_part(drift, lam, table, partial):
    fibres = drift.shape[1]
    velocity = split(drift[...] + lam[...], 3)

    for start in range(0, partial.shape[1], CHUNK):
        at = slice(start, start + CHUNK)
        partial[:, at] = join(dot(velocity, table[:fibres, at]), 3)


def rate_body(partial, extra, table, base, stacked, kind_row, rate_out):
    width, count = partial.shape
    kinds = stacked.shape[1] // width
    rows = extra.shape[1]
    for start in range(0, count, RATE_SIZE):
        at = slice(start, start + RATE_SIZE)
        far = join(dot(extra[...], table[base:base + rows, at]), 3)
        diff = (partial[:, at] + far).astype(BF16)
        kind = kind_row[:, at]
        none = jnp.zeros_like(diff)
        chosen = jnp.concatenate([jnp.where(kind == i, diff, none) for i in range(kinds)], axis=0)
        rate_out[:, at] = split(dot(stacked[...], chosen), 2)


def near_update(near_in, near_state, near_lam, rate, hot_near, outs):
    faces = []
    for pair in range(2):
        at = slice(pair * 256, pair * 256 + 256)
        rates = join(dot(rate[...], hot_near[:, at]), 2)
        lam = project(near_in[:, at] - OMEGA * (rates + near_state[1, :, at]))
        near_lam[:, at] = lam
        velocity = near_state[0, :, at] + lam
        faces += [velocity[:, i * LANES:(i + 1) * LANES] for i in range(2)]
    for out, block in zip(outs, outgoing(faces)):
        out[...] = block


def first_kernel(part0, part1, part2, part3, hot_land, lam_in, partial, table, stacked, kind,
                 hot_near, near_state, rate, near_lam, lam, out0, out1, out2, out3, extra):
    width, fibres = lam_in.shape
    quarter = width // 4
    parts = (part0, part1, part2, part3)
    blocks = incoming([part[:width, :] for part in parts])
    packed = incoming([part[width:, :] for part in parts])
    group = lane_group(quarter)
    arrived = []
    for q in range(4):
        block = jnp.zeros((quarter, LANES), F32)
        for face in range(4):
            rows = packed[face]
            moved = pltpu.roll(rows, (32 * (face - q)) % LANES, 1) if q != face else rows
            block = jnp.where(group == face, moved, block)
        arrived.append(block)
    arrived = jnp.concatenate(arrived, axis=0)
    near = len(blocks) * LANES
    for i, block in enumerate(blocks + [arrived]):
        extra[:, i * LANES:(i + 1) * LANES] = split(block, 3)
    rate_body(partial, extra, table, fibres, stacked, kind, rate)
    near_update(near_state[2], near_state, near_lam, rate, hot_near, (out0, out1, out2, out3))
    lam[...] = lam_in[...] + join(dot(extra[:, near:], hot_land[...]), 3)


def sweep_kernel(part0, part1, part2, part3, partial, table, stacked, kind,
                 hot_near, near_state, near_in, rate, near_lam, out0, out1, out2, out3, extra):
    parts = [part[...] for part in (part0, part1, part2, part3)]
    for i, block in enumerate(incoming(parts)):
        extra[:, i * LANES:(i + 1) * LANES] = split(block, 3)
    fibres = table.shape[0] - LANES - extra.shape[1]
    rate_body(partial, extra, table, fibres, stacked, kind, rate)
    near_update(near_in, near_state, near_lam, rate, hot_near, (out0, out1, out2, out3))


def update(rate, hot_first, lam_in, gap, lam, at, rates=None):
    total = join(dot(rate[...], hot_first[:, at]), 2)
    lam[:, at] = project(lam_in[:, at] - OMEGA * (total + gap[:, at]))
    if rates is not None:
        rates[:, at] = total


def own_kernel(rate, hot_first, lam_in, gap, drift, table, lam, partial):
    for start in range(0, lam.shape[1], CHUNK):
        update(rate, hot_first, lam_in, gap, lam, slice(start, start + CHUNK))
    own_part(drift, lam, table, partial)


def last_kernel(part0, part1, part2, part3, partial, table, stacked, kind,
                hot_first, lam_in, gap, lam_out, rates_out, rate, extra, lam, rates, sems):
    parts = [part[...] for part in (part0, part1, part2, part3)]
    for i, block in enumerate(incoming(parts)):
        extra[:, i * LANES:(i + 1) * LANES] = split(block, 3)
    fibres = table.shape[0] - LANES - extra.shape[1]
    rate_body(partial, extra, table, fibres, stacked, kind, rate)
    copies = []
    for n, start in enumerate(range(0, lam.shape[1], CHUNK)):
        at = slice(start, start + CHUNK)
        update(rate, hot_first, lam_in, gap, lam, at, rates)
        for i, (source, target) in enumerate(((lam, lam_out), (rates, rates_out))):
            copy = pltpu.make_async_copy(source.at[:, at], target.at[:, at], sems.at[n, i])
            copy.start()
            copies.append(copy)
    for copy in copies:
        copy.wait()


def call(kernel, outs, args, scalars=0, scratch=(), flops=0, space=pltpu.VMEM, out_space=pltpu.VMEM):
    scalar = pl.BlockSpec(memory_space=pltpu.SMEM)
    return pl.pallas_call(
        kernel,
        out_shape=[jax.ShapeDtypeStruct(s, d) for s, d in outs],
        in_specs=[scalar] * scalars + [pl.BlockSpec(memory_space=space)] * (len(args) - scalars),
        out_specs=[pl.BlockSpec(memory_space=out_space)] * len(outs),
        scratch_shapes=list(scratch),
        compiler_params=pltpu.CompilerParams(vmem_limit_bytes=VMEM_LIMIT),
        cost_estimate=pl.CostEstimate(flops=flops, bytes_accessed=4 << 20, transcendentals=0),
    )(*args)


def per_device(drift, warm, gap, mobility, near_list, send_slot, land_slot, contacts, live):
    width, fibres = drift.shape[0] * drift.shape[1], drift.shape[2]
    count = contacts.shape[1]
    near = near_list.shape[0] * near_list.shape[1]
    shape = drift.shape
    drift, warm, gap = (x.reshape(width, fibres) for x in (drift, warm, gap))
    total = fibres + near + LANES
    face = ((width, LANES), F32)
    big = ((width, fibres), F32)
    rate_shape = ((2 * width, count), BF16)
    near_shape = ((width, near), F32)
    partial_shape = ((width, count), F32)

    held = [pltpu.with_memory_space_constraint(x, pltpu.HBM) for x in (drift, warm, near_list, send_slot)]
    *sent, near_velocity = call(
        send_kernel, [((width + width // 4, LANES), F32)] * 4 + [near_shape], held, flops=2 << 30, space=pltpu.HBM,
        scratch=[pltpu.VMEM(x.shape, x.dtype) for x in held] + [pltpu.SemaphoreType.DMA((len(held),)), pltpu.VMEM((fibres, near), BF16), pltpu.VMEM((fibres, LANES), BF16)])
    halo = exchange(sent)
    table, hot_first, hot_near, hot_land, kind, partial, lam, near_state, stacked = call(
        setup_kernel,
        [((total, count), BF16), ((count, fibres), BF16), ((count, near), BF16), ((LANES, fibres), BF16),
         ((1, count), jnp.int32), partial_shape, big, ((3, width, near), F32),
         ((width, mobility.shape[0] * width), BF16)],
        (live, drift, warm, gap, near_list, send_slot, land_slot, contacts, mobility, near_velocity), scalars=1,
        flops=8 << 30)
    rate, near_lam, lam, *sent = call(
        first_kernel, [rate_shape, near_shape, big] + [face] * 4,
        (*halo, hot_land, lam, partial, table, stacked, kind, hot_near, near_state),
        scratch=[pltpu.VMEM((3 * width, near + LANES), BF16)], flops=4 << 30)
    for repeat in range(1, SWEEPS):
        halo = exchange(sent)
        lam, partial = call(own_kernel, [big, partial_shape], (rate, hot_first, lam, gap, drift, table),
                            flops=8 << 30)
        extra = pltpu.VMEM((3 * width, near), BF16)
        if repeat < SWEEPS - 1:
            rate, near_lam, *sent = call(
                sweep_kernel, [rate_shape, near_shape] + [face] * 4,
                (*halo, partial, table, stacked, kind, hot_near, near_state, near_lam),
                scratch=[extra], flops=4 << 30)
    lam, rates = call(
        last_kernel, [big, big],
        (*halo, partial, table, stacked, kind, hot_first, lam, gap),
        scratch=[pltpu.VMEM(*rate_shape), extra, pltpu.VMEM(*big), pltpu.VMEM(*big),
                 pltpu.SemaphoreType.DMA((fibres // CHUNK, 2))], flops=4 << 30, out_space=pltpu.HBM)
    return lam.reshape(shape), rates.reshape(shape)


def solution(mesh):
    both = ("grav", "cross")
    return jax.shard_map(
        per_device,
        mesh=mesh,
        in_specs=(
            P(None, None, both),
            P(None, None, both),
            P(None, None, both),
            P(),
            P(None, both),
            P(None, both),
            P(None, both),
            P(None, both),
            P(both),
        ),
        out_specs=(P(None, None, both), P(None, None, both)),
        check_vma=False,
    )
```

```python
import functools

import jax
import jax.numpy as jnp
from jax import lax
from jax.experimental import pallas as pl
from jax.experimental.pallas import tpu as pltpu
from jax.sharding import PartitionSpec as P

SWEEPS = 3
OMEGA = 0.5
FRICTION = 0.4
LANES = 128
CHUNK = 256
RATE_SIZE = 1024
VMEM_LIMIT = 24 * 1024 * 1024
F32 = jnp.float32
BF16 = jnp.bfloat16


def swap(x, axis, offset):
    count = lax.axis_size(axis)
    pairs = []
    for low in range(offset, count, 2):
        high = (low + 1) % count
        pairs += [(low, high), (high, low)]
    return lax.ppermute(x, axis, pairs)


def exchange(sent):
    steps = (("cross", 1), ("grav", 0), ("grav", 1), ("cross", 0))
    return [swap(block, *step) for block, step in zip(sent, steps)]


def odd(axis):
    return lax.rem(lax.axis_index(axis), 2) == 1


def outgoing(faces):
    c, g = odd("cross"), odd("grav")
    return (jnp.where(c, faces[3], faces[2]), jnp.where(g, faces[0], faces[1]),
            jnp.where(g, faces[1], faces[0]), jnp.where(c, faces[2], faces[3]))


def incoming(parts):
    c, g = odd("cross"), odd("grav")
    place = lax.axis_index("grav")
    below, above = jnp.where(g, parts[1], parts[2]), jnp.where(g, parts[2], parts[1])
    return [jnp.where(place == 0, 0.0, below), jnp.where(place == lax.axis_size("grav") - 1, 0.0, above),
            jnp.where(c, parts[3], parts[0]), jnp.where(c, parts[0], parts[3])]


def split(x, parts):
    out = []
    for _ in range(parts - 1):
        part = x.astype(BF16)
        out.append(part)
        x = x - part.astype(F32)
    out.append(x.astype(BF16))
    return jnp.concatenate(out, axis=0)


def join(y, parts):
    rows = y.shape[0] // parts
    total = y[(parts - 1) * rows:]
    for i in range(parts - 2, -1, -1):
        total = total + y[i * rows:(i + 1) * rows]
    return total


def dot(a, b):
    return jnp.dot(a, b, preferred_element_type=F32)


def iota(shape, dim):
    return lax.broadcasted_iota(jnp.int32, shape, dim)


def narrow(x, shape):
    return jnp.broadcast_to(x, shape).astype(jnp.int16)


def onehot(ids, wanted):
    shape = jnp.broadcast_shapes(ids.shape, wanted.shape)
    one, zero = jnp.ones(shape, BF16), jnp.zeros(shape, BF16)
    return jnp.where(narrow(ids, shape) == narrow(wanted, shape), one, zero)


def signed(ids, first, second):
    shape = jnp.broadcast_shapes(ids.shape, first.shape)
    one, zero = jnp.ones(shape, BF16), jnp.zeros(shape, BF16)
    ids = narrow(ids, shape)
    return jnp.where(ids == narrow(first, shape), one, jnp.where(ids == narrow(second, shape), -one, zero))


def column(row):
    size = row.shape[1]
    eye = iota((size, size), 0) == iota((size, size), 1)
    return jnp.sum(jnp.where(eye, row.astype(F32), 0.0), axis=1, keepdims=True).astype(jnp.int32)


def row_of(table):
    return jnp.concatenate([table[i:i + 1] for i in range(table.shape[0])], axis=1)


def project(trial):
    third = trial.shape[0] // 3
    normal = jnp.maximum(trial[:third], 0.0)
    bound = FRICTION * normal
    first = jnp.minimum(jnp.maximum(trial[third:2 * third], -bound), bound)
    second = jnp.minimum(jnp.maximum(trial[2 * third:], -bound), bound)
    return jnp.concatenate([normal, first, second], axis=0)


def lane_group(rows):
    return iota((rows, LANES), 1) // 32


def send_kernel(drift_hbm, warm_hbm, near_hbm, send_hbm, out0, out1, out2, out3, velocity_out,
                drift, warm, near, send, sems, hot_near, hot_send):
    copies = [pltpu.make_async_copy(source, target, sems.at[i]) for i, (source, target) in enumerate(
        ((near_hbm, near), (send_hbm, send), (warm_hbm, warm), (drift_hbm, drift)))]
    for copy in copies:
        copy.start()
    width, fibres = drift.shape
    quarter = width // 4
    slots = iota((fibres, LANES), 0)
    copies[0].wait()
    for face in range(4):
        hot_near[:, face * LANES:(face + 1) * LANES] = onehot(slots, near[face:face + 1, :])
    copies[1].wait()
    hot_send[...] = onehot(slots, row_of(send[...]))
    copies[2].wait()
    warm_now = warm[...]
    leaving = join(dot(split(warm_now, 3), hot_send[...]), 3)
    copies[3].wait()
    velocity = split(drift[...] + warm_now, 3)
    group = lane_group(quarter)
    blocks = []
    for pair in range(2):
        picked = join(dot(velocity, hot_near[:, pair * 256:pair * 256 + 256]), 3)
        velocity_out[:, pair * 256:pair * 256 + 256] = picked
        for i in range(2):
            face = 2 * pair + i
            packed = jnp.zeros((quarter, LANES), F32)
            for q in range(4):
                rows = leaving[q * quarter:(q + 1) * quarter]
                moved = pltpu.roll(rows, (32 * (q - face)) % LANES, 1) if q != face else rows
                packed = jnp.where(group == q, moved, packed)
            blocks.append((picked[:, i * LANES:(i + 1) * LANES], packed))
    for out, block, packed in zip((out0, out1, out2, out3), outgoing([b[0] for b in blocks]),
                                  outgoing([b[1] for b in blocks])):
        out[:width, :] = block
        out[width:, :] = packed


def setup_kernel(live, drift, warm, gap, near, send, land, contacts, mobility, near_velocity,
                 table, hot_first, hot_near, hot_land, kind, partial, lam, near_state, stacked):
    width, fibres = drift.shape
    count = contacts.shape[1]
    total = table.shape[0]

    land_row = row_of(land[...])
    land_column = column(land_row)

    for start in range(0, count, CHUNK):
        at = slice(start, start + CHUNK)
        alive = start + iota((1, CHUNK), 1) < live[0]
        first = jnp.where(alive, contacts[0:1, at], -1)
        second = jnp.where(alive, contacts[1:2, at], -1)
        for row in range(0, total - LANES, LANES):
            table[row:row + LANES, at] = signed(row + iota((LANES, CHUNK), 0), first, second)
        table[total - LANES:, at] = signed(land_column, first, second)

    for start in range(0, count, LANES):
        at = slice(start, start + LANES)
        first = column(contacts[0:1, at])
        hot_first[at, :] = onehot(first, iota((LANES, fibres), 1))
        for face in range(4):
            hot_near[at, face * LANES:(face + 1) * LANES] = onehot(first, near[face:face + 1, :])

    stacked[...] = jnp.concatenate([mobility[i] for i in range(mobility.shape[0])], axis=1)

    taken = (column(row_of(send[...])) == iota((LANES, fibres), 1)) | (land_column == iota((LANES, fibres), 1))
    keep = jnp.max(jnp.where(taken, 1.0, 0.0), axis=0, keepdims=True) < 0.5
    hot_land[...] = onehot(land_column, iota((LANES, fibres), 1))
    kind[...] = contacts[2:3, :]
    lam_now = jnp.where(keep, warm[...], 0.0)
    lam[...] = lam_now

    slots = iota((fibres, LANES), 0)
    for pair in range(2):
        hot = jnp.concatenate([onehot(slots, near[2 * pair + i:2 * pair + i + 1, :]) for i in range(2)], axis=1)
        at = slice(pair * 256, pair * 256 + 256)
        near_warm = join(dot(split(warm[...], 3), hot), 3)
        near_state[0, :, at] = near_velocity[:, at] - near_warm
        near_state[1, :, at] = join(dot(split(gap[...], 3), hot), 3)
        near_state[2, :, at] = near_warm

    own_part(drift, lam, table, partial)


def own_part(drift, lam, table, partial):
    fibres = drift.shape[1]
    velocity = split(drift[...] + lam[...], 3)

    for start in range(0, partial.shape[1], CHUNK):
        at = slice(start, start + CHUNK)
        partial[:, at] = join(dot(velocity, table[:fibres, at]), 3)


def rate_body(partial, extra, table, base, stacked, kind_row, rate_out):
    width, count = partial.shape
    kinds = stacked.shape[1] // width
    rows = extra.shape[1]
    for start in range(0, count, RATE_SIZE):
        at = slice(start, start + RATE_SIZE)
        far = join(dot(extra[...], table[base:base + rows, at]), 3)
        diff = (partial[:, at] + far).astype(BF16)
        kind = kind_row[:, at]
        none = jnp.zeros_like(diff)
        chosen = jnp.concatenate([jnp.where(kind == i, diff, none) for i in range(kinds)], axis=0)
        rate_out[:, at] = split(dot(stacked[...], chosen), 2)


def near_update(near_in, near_state, near_lam, rate, hot_near, outs):
    faces = []
    for pair in range(2):
        at = slice(pair * 256, pair * 256 + 256)
        rates = join(dot(rate[...], hot_near[:, at]), 2)
        lam = project(near_in[:, at] - OMEGA * (rates + near_state[1, :, at]))
        near_lam[:, at] = lam
        velocity = near_state[0, :, at] + lam
        faces += [velocity[:, i * LANES:(i + 1) * LANES] for i in range(2)]
    for out, block in zip(outs, outgoing(faces)):
        out[...] = block


def first_kernel(part0, part1, part2, part3, hot_land, lam_in, partial, table, stacked, kind,
                 hot_near, near_state, rate, near_lam, lam, out0, out1, out2, out3, extra):
    width, fibres = lam_in.shape
    quarter = width // 4
    parts = (part0, part1, part2, part3)
    blocks = incoming([part[:width, :] for part in parts])
    packed = incoming([part[width:, :] for part in parts])
    group = lane_group(quarter)
    arrived = []
    for q in range(4):
        block = jnp.zeros((quarter, LANES), F32)
        for face in range(4):
            rows = packed[face]
            moved = pltpu.roll(rows, (32 * (face - q)) % LANES, 1) if q != face else rows
            block = jnp.where(group == face, moved, block)
        arrived.append(block)
    arrived = jnp.concatenate(arrived, axis=0)
    near = len(blocks) * LANES
    for i, block in enumerate(blocks + [arrived]):
        extra[:, i * LANES:(i + 1) * LANES] = split(block, 3)
    rate_body(partial, extra, table, fibres, stacked, kind, rate)
    near_update(near_state[2], near_state, near_lam, rate, hot_near, (out0, out1, out2, out3))
    lam[...] = lam_in[...] + join(dot(extra[:, near:], hot_land[...]), 3)


def sweep_kernel(part0, part1, part2, part3, partial, table, stacked, kind,
                 hot_near, near_state, near_in, rate, near_lam, out0, out1, out2, out3, extra):
    parts = [part[...] for part in (part0, part1, part2, part3)]
    for i, block in enumerate(incoming(parts)):
        extra[:, i * LANES:(i + 1) * LANES] = split(block, 3)
    fibres = table.shape[0] - LANES - extra.shape[1]
    rate_body(partial, extra, table, fibres, stacked, kind, rate)
    near_update(near_in, near_state, near_lam, rate, hot_near, (out0, out1, out2, out3))


def update(rate, hot_first, lam_in, gap, lam, at, rates=None):
    total = join(dot(rate[...], hot_first[:, at]), 2)
    lam[:, at] = project(lam_in[:, at] - OMEGA * (total + gap[:, at]))
    if rates is not None:
        rates[:, at] = total


def own_kernel(rate, hot_first, lam_in, gap, drift, table, lam, partial):
    for start in range(0, lam.shape[1], CHUNK):
        update(rate, hot_first, lam_in, gap, lam, slice(start, start + CHUNK))
    own_part(drift, lam, table, partial)


def last_kernel(part0, part1, part2, part3, partial, table, stacked, kind,
                hot_first, lam_in, gap, lam_out, rates_out, rate, extra, lam, rates, sems):
    parts = [part[...] for part in (part0, part1, part2, part3)]
    for i, block in enumerate(incoming(parts)):
        extra[:, i * LANES:(i + 1) * LANES] = split(block, 3)
    fibres = table.shape[0] - LANES - extra.shape[1]
    rate_body(partial, extra, table, fibres, stacked, kind, rate)
    copies = []
    for n, start in enumerate(range(0, lam.shape[1], CHUNK)):
        at = slice(start, start + CHUNK)
        update(rate, hot_first, lam_in, gap, lam, at, rates)
        for i, (source, target) in enumerate(((lam, lam_out), (rates, rates_out))):
            copy = pltpu.make_async_copy(source.at[:, at], target.at[:, at], sems.at[n, i])
            copy.start()
            copies.append(copy)
    for copy in copies:
        copy.wait()


def call(kernel, outs, args, scalars=0, scratch=(), flops=0, space=pltpu.VMEM, out_space=pltpu.VMEM):
    scalar = pl.BlockSpec(memory_space=pltpu.SMEM)
    return pl.pallas_call(
        kernel,
        out_shape=[jax.ShapeDtypeStruct(s, d) for s, d in outs],
        in_specs=[scalar] * scalars + [pl.BlockSpec(memory_space=space)] * (len(args) - scalars),
        out_specs=[pl.BlockSpec(memory_space=out_space)] * len(outs),
        scratch_shapes=list(scratch),
        compiler_params=pltpu.CompilerParams(vmem_limit_bytes=VMEM_LIMIT),
        cost_estimate=pl.CostEstimate(flops=flops, bytes_accessed=4 << 20, transcendentals=0),
    )(*args)


def per_device(drift, warm, gap, mobility, near_list, send_slot, land_slot, contacts, live):
    width, fibres = drift.shape[0] * drift.shape[1], drift.shape[2]
    count = contacts.shape[1]
    near = near_list.shape[0] * near_list.shape[1]
    shape = drift.shape
    drift, warm, gap = (x.reshape(width, fibres) for x in (drift, warm, gap))
    total = fibres + near + LANES
    face = ((width, LANES), F32)
    big = ((width, fibres), F32)
    rate_shape = ((2 * width, count), BF16)
    near_shape = ((width, near), F32)
    partial_shape = ((width, count), F32)

    held = [pltpu.with_memory_space_constraint(x, pltpu.HBM) for x in (drift, warm, near_list, send_slot)]
    *sent, near_velocity = call(
        send_kernel, [((width + width // 4, LANES), F32)] * 4 + [near_shape], held, flops=2 << 30, space=pltpu.HBM,
        scratch=[pltpu.VMEM(x.shape, x.dtype) for x in held] + [pltpu.SemaphoreType.DMA((len(held),)), pltpu.VMEM((fibres, near), BF16), pltpu.VMEM((fibres, LANES), BF16)])
    halo = exchange(sent)
    table, hot_first, hot_near, hot_land, kind, partial, lam, near_state, stacked = call(
        setup_kernel,
        [((total, count), BF16), ((count, fibres), BF16), ((count, near), BF16), ((LANES, fibres), BF16),
         ((1, count), jnp.int32), partial_shape, big, ((3, width, near), F32),
         ((width, mobility.shape[0] * width), BF16)],
        (live, drift, warm, gap, near_list, send_slot, land_slot, contacts, mobility, near_velocity), scalars=1,
        flops=8 << 30)
    rate, near_lam, lam, *sent = call(
        first_kernel, [rate_shape, near_shape, big] + [face] * 4,
        (*halo, hot_land, lam, partial, table, stacked, kind, hot_near, near_state),
        scratch=[pltpu.VMEM((3 * width, near + LANES), BF16)], flops=4 << 30)
    for repeat in range(1, SWEEPS):
        halo = exchange(sent)
        lam, partial = call(own_kernel, [big, partial_shape], (rate, hot_first, lam, gap, drift, table),
                            flops=8 << 30)
        extra = pltpu.VMEM((3 * width, near), BF16)
        if repeat < SWEEPS - 1:
            rate, near_lam, *sent = call(
                sweep_kernel, [rate_shape, near_shape] + [face] * 4,
                (*halo, partial, table, stacked, kind, hot_near, near_state, near_lam),
                scratch=[extra], flops=4 << 30)
    lam, rates = call(
        last_kernel, [big, big],
        (*halo, partial, table, stacked, kind, hot_first, lam, gap),
        scratch=[pltpu.VMEM(*rate_shape), extra, pltpu.VMEM(*big), pltpu.VMEM(*big),
                 pltpu.SemaphoreType.DMA((fibres // CHUNK, 2))], flops=4 << 30, out_space=pltpu.HBM)
    return lam.reshape(shape), rates.reshape(shape)


def solution(mesh):
    both = ("grav", "cross")
    return jax.shard_map(
        per_device,
        mesh=mesh,
        in_specs=(
            P(None, None, both),
            P(None, None, both),
            P(None, None, both),
            P(),
            P(None, both),
            P(None, both),
            P(None, both),
            P(None, both),
            P(both),
        ),
        out_specs=(P(None, None, both), P(None, None, both)),
        check_vma=False,
    )
```

```python
import functools

import jax
import jax.numpy as jnp
from jax import lax
from jax.experimental import pallas as pl
from jax.experimental.pallas import tpu as pltpu
from jax.sharding import PartitionSpec as P

SWEEPS = 3
OMEGA = 0.5
FRICTION = 0.4
LANES = 128
CHUNK = 256
RATE_SIZE = 1024
VMEM_LIMIT = 24 * 1024 * 1024
F32 = jnp.float32
BF16 = jnp.bfloat16


def swap(x, axis, offset):
    count = lax.axis_size(axis)
    pairs = []
    for low in range(offset, count, 2):
        high = (low + 1) % count
        pairs += [(low, high), (high, low)]
    return lax.ppermute(x, axis, pairs)


STEPS = (("cross", 1), ("grav", 0), ("grav", 1), ("cross", 0))
CHIP_FIRST = (3, 0, 1, 2)
CHIP_LAST = (0, 1, 2, 3)


def exchange(sent, order):
    return [swap(sent[step], *STEPS[step]) for step in order]


def odd(axis):
    return lax.rem(lax.axis_index(axis), 2) == 1


def outgoing(faces):
    c, g = odd("cross"), odd("grav")
    return (jnp.where(c, faces[3], faces[2]), jnp.where(g, faces[0], faces[1]),
            jnp.where(g, faces[1], faces[0]), jnp.where(c, faces[2], faces[3]))


def incoming(parts, order):
    parts = [parts[order.index(step)] for step in range(len(order))]
    c, g = odd("cross"), odd("grav")
    place = lax.axis_index("grav")
    below, above = jnp.where(g, parts[1], parts[2]), jnp.where(g, parts[2], parts[1])
    return [jnp.where(place == 0, 0.0, below), jnp.where(place == lax.axis_size("grav") - 1, 0.0, above),
            jnp.where(c, parts[3], parts[0]), jnp.where(c, parts[0], parts[3])]


def split(x, parts):
    out = []
    for _ in range(parts - 1):
        part = x.astype(BF16)
        out.append(part)
        x = x - part.astype(F32)
    out.append(x.astype(BF16))
    return jnp.concatenate(out, axis=0)


def join(y, parts):
    rows = y.shape[0] // parts
    total = y[(parts - 1) * rows:]
    for i in range(parts - 2, -1, -1):
        total = total + y[i * rows:(i + 1) * rows]
    return total


def dot(a, b):
    return jnp.dot(a, b, preferred_element_type=F32)


def iota(shape, dim):
    return lax.broadcasted_iota(jnp.int32, shape, dim)


def narrow(x, shape):
    return jnp.broadcast_to(x, shape).astype(jnp.int16)


def onehot(ids, wanted):
    shape = jnp.broadcast_shapes(ids.shape, wanted.shape)
    one, zero = jnp.ones(shape, BF16), jnp.zeros(shape, BF16)
    return jnp.where(narrow(ids, shape) == narrow(wanted, shape), one, zero)


def signed(ids, first, second):
    shape = jnp.broadcast_shapes(ids.shape, first.shape)
    one, zero = jnp.ones(shape, BF16), jnp.zeros(shape, BF16)
    ids = narrow(ids, shape)
    return jnp.where(ids == narrow(first, shape), one, jnp.where(ids == narrow(second, shape), -one, zero))


def column(row):
    size = row.shape[1]
    eye = iota((size, size), 0) == iota((size, size), 1)
    return jnp.sum(jnp.where(eye, row.astype(F32), 0.0), axis=1, keepdims=True).astype(jnp.int32)


def row_of(table):
    return jnp.concatenate([table[i:i + 1] for i in range(table.shape[0])], axis=1)


def project(trial):
    third = trial.shape[0] // 3
    normal = jnp.maximum(trial[:third], 0.0)
    bound = FRICTION * normal
    first = jnp.minimum(jnp.maximum(trial[third:2 * third], -bound), bound)
    second = jnp.minimum(jnp.maximum(trial[2 * third:], -bound), bound)
    return jnp.concatenate([normal, first, second], axis=0)


def lane_group(rows):
    return iota((rows, LANES), 1) // 32


def send_kernel(drift_hbm, warm_hbm, near_hbm, send_hbm, out0, out1, out2, out3, velocity_out,
                drift, warm, near, send, sems, hot_near, hot_send):
    copies = [pltpu.make_async_copy(source, target, sems.at[i]) for i, (source, target) in enumerate(
        ((near_hbm, near), (send_hbm, send), (warm_hbm, warm), (drift_hbm, drift)))]
    for copy in copies:
        copy.start()
    width, fibres = drift.shape
    quarter = width // 4
    slots = iota((fibres, LANES), 0)
    copies[0].wait()
    for face in range(4):
        hot_near[:, face * LANES:(face + 1) * LANES] = onehot(slots, near[face:face + 1, :])
    copies[1].wait()
    hot_send[...] = onehot(slots, row_of(send[...]))
    copies[2].wait()
    warm_now = warm[...]
    leaving = join(dot(split(warm_now, 3), hot_send[...]), 3)
    copies[3].wait()
    velocity = split(drift[...] + warm_now, 3)
    group = lane_group(quarter)
    blocks = []
    for pair in range(2):
        picked = join(dot(velocity, hot_near[:, pair * 256:pair * 256 + 256]), 3)
        velocity_out[:, pair * 256:pair * 256 + 256] = picked
        for i in range(2):
            face = 2 * pair + i
            packed = jnp.zeros((quarter, LANES), F32)
            for q in range(4):
                rows = leaving[q * quarter:(q + 1) * quarter]
                moved = pltpu.roll(rows, (32 * (q - face)) % LANES, 1) if q != face else rows
                packed = jnp.where(group == q, moved, packed)
            blocks.append((picked[:, i * LANES:(i + 1) * LANES], packed))
    for out, block, packed in zip((out0, out1, out2, out3), outgoing([b[0] for b in blocks]),
                                  outgoing([b[1] for b in blocks])):
        out[:width, :] = block
        out[width:, :] = packed


def setup_kernel(live, drift, warm, gap, near, send, land, contacts, mobility, near_velocity,
                 table, hot_first, hot_near, hot_land, kind, partial, lam, near_state, stacked):
    width, fibres = drift.shape
    count = contacts.shape[1]
    total = table.shape[0]

    land_row = row_of(land[...])
    land_column = column(land_row)

    for start in range(0, count, CHUNK):
        at = slice(start, start + CHUNK)
        alive = start + iota((1, CHUNK), 1) < live[0]
        first = jnp.where(alive, contacts[0:1, at], -1)
        second = jnp.where(alive, contacts[1:2, at], -1)
        for row in range(0, total - LANES, LANES):
            table[row:row + LANES, at] = signed(row + iota((LANES, CHUNK), 0), first, second)
        table[total - LANES:, at] = signed(land_column, first, second)

    for start in range(0, count, LANES):
        at = slice(start, start + LANES)
        first = column(contacts[0:1, at])
        hot_first[at, :] = onehot(first, iota((LANES, fibres), 1))
        for face in range(4):
            hot_near[at, face * LANES:(face + 1) * LANES] = onehot(first, near[face:face + 1, :])

    stacked[...] = jnp.concatenate([mobility[i] for i in range(mobility.shape[0])], axis=1)

    taken = (column(row_of(send[...])) == iota((LANES, fibres), 1)) | (land_column == iota((LANES, fibres), 1))
    keep = jnp.max(jnp.where(taken, 1.0, 0.0), axis=0, keepdims=True) < 0.5
    hot_land[...] = onehot(land_column, iota((LANES, fibres), 1))
    kind[...] = contacts[2:3, :]
    lam_now = jnp.where(keep, warm[...], 0.0)
    lam[...] = lam_now

    slots = iota((fibres, LANES), 0)
    for pair in range(2):
        hot = jnp.concatenate([onehot(slots, near[2 * pair + i:2 * pair + i + 1, :]) for i in range(2)], axis=1)
        at = slice(pair * 256, pair * 256 + 256)
        near_warm = join(dot(split(warm[...], 3), hot), 3)
        near_state[0, :, at] = near_velocity[:, at] - near_warm
        near_state[1, :, at] = join(dot(split(gap[...], 3), hot), 3)
        near_state[2, :, at] = near_warm

    own_part(drift, lam, table, partial)


def own_part(drift, lam, table, partial):
    fibres = drift.shape[1]
    velocity = split(drift[...] + lam[...], 3)

    for start in range(0, partial.shape[1], CHUNK):
        at = slice(start, start + CHUNK)
        partial[:, at] = join(dot(velocity, table[:fibres, at]), 3)


def rate_body(partial, extra, table, base, stacked, kind_row, rate_out):
    width, count = partial.shape
    kinds = stacked.shape[1] // width
    rows = extra.shape[1]
    for start in range(0, count, RATE_SIZE):
        at = slice(start, start + RATE_SIZE)
        far = join(dot(extra[...], table[base:base + rows, at]), 3)
        diff = (partial[:, at] + far).astype(BF16)
        kind = kind_row[:, at]
        none = jnp.zeros_like(diff)
        chosen = jnp.concatenate([jnp.where(kind == i, diff, none) for i in range(kinds)], axis=0)
        rate_out[:, at] = split(dot(stacked[...], chosen), 2)


def near_update(near_in, near_state, near_lam, rate, hot_near, outs):
    faces = []
    for pair in range(2):
        at = slice(pair * 256, pair * 256 + 256)
        rates = join(dot(rate[...], hot_near[:, at]), 2)
        lam = project(near_in[:, at] - OMEGA * (rates + near_state[1, :, at]))
        near_lam[:, at] = lam
        velocity = near_state[0, :, at] + lam
        faces += [velocity[:, i * LANES:(i + 1) * LANES] for i in range(2)]
    for out, block in zip(outs, outgoing(faces)):
        out[...] = block


def first_kernel(part0, part1, part2, part3, hot_land, lam_in, partial, table, stacked, kind,
                 hot_near, near_state, rate, near_lam, lam, out0, out1, out2, out3, extra):
    width, fibres = lam_in.shape
    quarter = width // 4
    parts = (part0, part1, part2, part3)
    blocks = incoming([part[:width, :] for part in parts], CHIP_FIRST)
    packed = incoming([part[width:, :] for part in parts], CHIP_FIRST)
    group = lane_group(quarter)
    arrived = []
    for q in range(4):
        block = jnp.zeros((quarter, LANES), F32)
        for face in range(4):
            rows = packed[face]
            moved = pltpu.roll(rows, (32 * (face - q)) % LANES, 1) if q != face else rows
            block = jnp.where(group == face, moved, block)
        arrived.append(block)
    arrived = jnp.concatenate(arrived, axis=0)
    near = len(blocks) * LANES
    for i, block in enumerate(blocks + [arrived]):
        extra[:, i * LANES:(i + 1) * LANES] = split(block, 3)
    rate_body(partial, extra, table, fibres, stacked, kind, rate)
    near_update(near_state[2], near_state, near_lam, rate, hot_near, (out0, out1, out2, out3))
    lam[...] = lam_in[...] + join(dot(extra[:, near:], hot_land[...]), 3)


def sweep_kernel(part0, part1, part2, part3, partial, table, stacked, kind,
                 hot_near, near_state, near_in, rate, near_lam, out0, out1, out2, out3, extra):
    parts = [part[...] for part in (part0, part1, part2, part3)]
    for i, block in enumerate(incoming(parts, CHIP_LAST)):
        extra[:, i * LANES:(i + 1) * LANES] = split(block, 3)
    fibres = table.shape[0] - LANES - extra.shape[1]
    rate_body(partial, extra, table, fibres, stacked, kind, rate)
    near_update(near_in, near_state, near_lam, rate, hot_near, (out0, out1, out2, out3))


def update(rate, hot_first, lam_in, gap, lam, at, rates=None):
    total = join(dot(rate[...], hot_first[:, at]), 2)
    lam[:, at] = project(lam_in[:, at] - OMEGA * (total + gap[:, at]))
    if rates is not None:
        rates[:, at] = total


def own_kernel(rate, hot_first, lam_in, gap, drift, table, lam, partial):
    for start in range(0, lam.shape[1], CHUNK):
        update(rate, hot_first, lam_in, gap, lam, slice(start, start + CHUNK))
    own_part(drift, lam, table, partial)


def last_kernel(part0, part1, part2, part3, partial, table, stacked, kind,
                hot_first, lam_in, gap, lam_out, rates_out, rate, extra, lam, rates, sems):
    parts = [part[...] for part in (part0, part1, part2, part3)]
    for i, block in enumerate(incoming(parts, CHIP_FIRST)):
        extra[:, i * LANES:(i + 1) * LANES] = split(block, 3)
    fibres = table.shape[0] - LANES - extra.shape[1]
    rate_body(partial, extra, table, fibres, stacked, kind, rate)
    copies = []
    for n, start in enumerate(range(0, lam.shape[1], CHUNK)):
        at = slice(start, start + CHUNK)
        update(rate, hot_first, lam_in, gap, lam, at, rates)
        for i, (source, target) in enumerate(((lam, lam_out), (rates, rates_out))):
            copy = pltpu.make_async_copy(source.at[:, at], target.at[:, at], sems.at[n, i])
            copy.start()
            copies.append(copy)
    for copy in copies:
        copy.wait()


def call(kernel, outs, args, scalars=0, scratch=(), flops=0, space=pltpu.VMEM, out_space=pltpu.VMEM):
    scalar = pl.BlockSpec(memory_space=pltpu.SMEM)
    return pl.pallas_call(
        kernel,
        out_shape=[jax.ShapeDtypeStruct(s, d) for s, d in outs],
        in_specs=[scalar] * scalars + [pl.BlockSpec(memory_space=space)] * (len(args) - scalars),
        out_specs=[pl.BlockSpec(memory_space=out_space)] * len(outs),
        scratch_shapes=list(scratch),
        compiler_params=pltpu.CompilerParams(vmem_limit_bytes=VMEM_LIMIT),
        cost_estimate=pl.CostEstimate(flops=flops, bytes_accessed=4 << 20, transcendentals=0),
    )(*args)


def per_device(drift, warm, gap, mobility, near_list, send_slot, land_slot, contacts, live):
    width, fibres = drift.shape[0] * drift.shape[1], drift.shape[2]
    count = contacts.shape[1]
    near = near_list.shape[0] * near_list.shape[1]
    shape = drift.shape
    drift, warm, gap = (x.reshape(width, fibres) for x in (drift, warm, gap))
    total = fibres + near + LANES
    face = ((width, LANES), F32)
    big = ((width, fibres), F32)
    rate_shape = ((2 * width, count), BF16)
    near_shape = ((width, near), F32)
    partial_shape = ((width, count), F32)

    held = [pltpu.with_memory_space_constraint(x, pltpu.HBM) for x in (drift, warm, near_list, send_slot)]
    *sent, near_velocity = call(
        send_kernel, [((width + width // 4, LANES), F32)] * 4 + [near_shape], held, flops=2 << 30, space=pltpu.HBM,
        scratch=[pltpu.VMEM(x.shape, x.dtype) for x in held] + [pltpu.SemaphoreType.DMA((len(held),)), pltpu.VMEM((fibres, near), BF16), pltpu.VMEM((fibres, LANES), BF16)])
    halo = exchange(sent, CHIP_FIRST)
    table, hot_first, hot_near, hot_land, kind, partial, lam, near_state, stacked = call(
        setup_kernel,
        [((total, count), BF16), ((count, fibres), BF16), ((count, near), BF16), ((LANES, fibres), BF16),
         ((1, count), jnp.int32), partial_shape, big, ((3, width, near), F32),
         ((width, mobility.shape[0] * width), BF16)],
        (live, drift, warm, gap, near_list, send_slot, land_slot, contacts, mobility, near_velocity), scalars=1,
        flops=8 << 30)
    rate, near_lam, lam, *sent = call(
        first_kernel, [rate_shape, near_shape, big] + [face] * 4,
        (*halo, hot_land, lam, partial, table, stacked, kind, hot_near, near_state),
        scratch=[pltpu.VMEM((3 * width, near + LANES), BF16)], flops=4 << 30)
    for repeat in range(1, SWEEPS):
        halo = exchange(sent, CHIP_LAST if repeat < SWEEPS - 1 else CHIP_FIRST)
        lam, partial = call(own_kernel, [big, partial_shape], (rate, hot_first, lam, gap, drift, table),
                            flops=8 << 30)
        extra = pltpu.VMEM((3 * width, near), BF16)
        if repeat < SWEEPS - 1:
            rate, near_lam, *sent = call(
                sweep_kernel, [rate_shape, near_shape] + [face] * 4,
                (*halo, partial, table, stacked, kind, hot_near, near_state, near_lam),
                scratch=[extra], flops=4 << 30)
    lam, rates = call(
        last_kernel, [big, big],
        (*halo, partial, table, stacked, kind, hot_first, lam, gap),
        scratch=[pltpu.VMEM(*rate_shape), extra, pltpu.VMEM(*big), pltpu.VMEM(*big),
                 pltpu.SemaphoreType.DMA((fibres // CHUNK, 2))], flops=4 << 30, out_space=pltpu.HBM)
    return lam.reshape(shape), rates.reshape(shape)


def solution(mesh):
    both = ("grav", "cross")
    return jax.shard_map(
        per_device,
        mesh=mesh,
        in_specs=(
            P(None, None, both),
            P(None, None, both),
            P(None, None, both),
            P(),
            P(None, both),
            P(None, both),
            P(None, both),
            P(None, both),
            P(both),
        ),
        out_specs=(P(None, None, both), P(None, None, both)),
        check_vma=False,
    )
```

```python
import functools

import jax
import jax.numpy as jnp
from jax import lax
from jax.experimental import pallas as pl
from jax.experimental.pallas import tpu as pltpu
from jax.sharding import PartitionSpec as P

SWEEPS = 3
OMEGA = 0.5
FRICTION = 0.4
LANES = 128
CHUNK = 256
RATE_SIZE = 1024
VMEM_LIMIT = 24 * 1024 * 1024
F32 = jnp.float32
BF16 = jnp.bfloat16


def swap(x, axis, offset):
    count = lax.axis_size(axis)
    pairs = []
    for low in range(offset, count, 2):
        high = (low + 1) % count
        pairs += [(low, high), (high, low)]
    return lax.ppermute(x, axis, pairs)


STEPS = (("cross", 1), ("grav", 0), ("grav", 1), ("cross", 0))
CHIP_FIRST = (3, 0, 1, 2)
CHIP_LAST = (0, 1, 2, 3)


def exchange(sent, order):
    return [swap(sent[step], *STEPS[step]) for step in order]


def odd(axis):
    return lax.rem(lax.axis_index(axis), 2) == 1


def outgoing(faces):
    c, g = odd("cross"), odd("grav")
    return (jnp.where(c, faces[3], faces[2]), jnp.where(g, faces[0], faces[1]),
            jnp.where(g, faces[1], faces[0]), jnp.where(c, faces[2], faces[3]))


def incoming(parts, order):
    parts = [parts[order.index(step)] for step in range(len(order))]
    c, g = odd("cross"), odd("grav")
    place = lax.axis_index("grav")
    below, above = jnp.where(g, parts[1], parts[2]), jnp.where(g, parts[2], parts[1])
    return [jnp.where(place == 0, 0.0, below), jnp.where(place == lax.axis_size("grav") - 1, 0.0, above),
            jnp.where(c, parts[3], parts[0]), jnp.where(c, parts[0], parts[3])]


def split(x, parts):
    out = []
    for _ in range(parts - 1):
        part = x.astype(BF16)
        out.append(part)
        x = x - part.astype(F32)
    out.append(x.astype(BF16))
    return jnp.concatenate(out, axis=0)


def join(y, parts):
    rows = y.shape[0] // parts
    total = y[(parts - 1) * rows:]
    for i in range(parts - 2, -1, -1):
        total = total + y[i * rows:(i + 1) * rows]
    return total


def dot(a, b):
    return jnp.dot(a, b, preferred_element_type=F32)


def iota(shape, dim):
    return lax.broadcasted_iota(jnp.int32, shape, dim)


def narrow(x, shape):
    return jnp.broadcast_to(x, shape).astype(jnp.int16)


def onehot(ids, wanted):
    shape = jnp.broadcast_shapes(ids.shape, wanted.shape)
    one, zero = jnp.ones(shape, BF16), jnp.zeros(shape, BF16)
    return jnp.where(narrow(ids, shape) == narrow(wanted, shape), one, zero)


def signed(ids, first, second):
    shape = jnp.broadcast_shapes(ids.shape, first.shape)
    one, zero = jnp.ones(shape, BF16), jnp.zeros(shape, BF16)
    ids = narrow(ids, shape)
    return jnp.where(ids == narrow(first, shape), one, jnp.where(ids == narrow(second, shape), -one, zero))


def column(row):
    size = row.shape[1]
    eye = iota((size, size), 0) == iota((size, size), 1)
    return jnp.sum(jnp.where(eye, row.astype(F32), 0.0), axis=1, keepdims=True).astype(jnp.int32)


def row_of(table):
    return jnp.concatenate([table[i:i + 1] for i in range(table.shape[0])], axis=1)


def project(trial):
    third = trial.shape[0] // 3
    normal = jnp.maximum(trial[:third], 0.0)
    bound = FRICTION * normal
    first = jnp.minimum(jnp.maximum(trial[third:2 * third], -bound), bound)
    second = jnp.minimum(jnp.maximum(trial[2 * third:], -bound), bound)
    return jnp.concatenate([normal, first, second], axis=0)


def lane_group(rows):
    return iota((rows, LANES), 1) // 32


def send_kernel(drift_hbm, warm_hbm, near_hbm, send_hbm, out0, out1, out2, out3, velocity_out,
                drift, warm, near, send, sems, hot_near, hot_send):
    copies = [pltpu.make_async_copy(source, target, sems.at[i]) for i, (source, target) in enumerate(
        ((near_hbm, near), (send_hbm, send), (warm_hbm, warm), (drift_hbm, drift)))]
    for copy in copies:
        copy.start()
    width, fibres = drift.shape
    quarter = width // 4
    slots = iota((fibres, LANES), 0)
    copies[0].wait()
    for face in range(4):
        hot_near[:, face * LANES:(face + 1) * LANES] = onehot(slots, near[face:face + 1, :])
    copies[1].wait()
    hot_send[...] = onehot(slots, row_of(send[...]))
    copies[2].wait()
    warm_now = warm[...]
    leaving = join(dot(split(warm_now, 3), hot_send[...]), 3)
    copies[3].wait()
    velocity = split(drift[...] + warm_now, 3)
    group = lane_group(quarter)
    blocks = []
    for pair in range(2):
        picked = join(dot(velocity, hot_near[:, pair * 256:pair * 256 + 256]), 3)
        velocity_out[:, pair * 256:pair * 256 + 256] = picked
        for i in range(2):
            face = 2 * pair + i
            packed = jnp.zeros((quarter, LANES), F32)
            for q in range(4):
                rows = leaving[q * quarter:(q + 1) * quarter]
                moved = pltpu.roll(rows, (32 * (q - face)) % LANES, 1) if q != face else rows
                packed = jnp.where(group == q, moved, packed)
            blocks.append((picked[:, i * LANES:(i + 1) * LANES], packed))
    for out, block, packed in zip((out0, out1, out2, out3), outgoing([b[0] for b in blocks]),
                                  outgoing([b[1] for b in blocks])):
        out[:width, :] = block
        out[width:, :] = packed


def setup_kernel(live, drift, warm, gap, near, send, land, contacts, mobility, near_velocity,
                 table, hot_first, hot_near, hot_land, kind, partial, lam, near_state, stacked):
    width, fibres = drift.shape
    count = contacts.shape[1]
    total = table.shape[0]

    land_row = row_of(land[...])
    land_column = column(land_row)

    for start in range(0, count, CHUNK):
        at = slice(start, start + CHUNK)
        alive = start + iota((1, CHUNK), 1) < live[0]
        first = jnp.where(alive, contacts[0:1, at], -1)
        second = jnp.where(alive, contacts[1:2, at], -1)
        for row in range(0, total - LANES, LANES):
            table[row:row + LANES, at] = signed(row + iota((LANES, CHUNK), 0), first, second)
        table[total - LANES:, at] = signed(land_column, first, second)

    for start in range(0, count, LANES):
        at = slice(start, start + LANES)
        first = column(contacts[0:1, at])
        hot_first[at, :] = onehot(first, iota((LANES, fibres), 1))
        for face in range(4):
            hot_near[at, face * LANES:(face + 1) * LANES] = onehot(first, near[face:face + 1, :])

    stacked[...] = jnp.concatenate([mobility[i] for i in range(mobility.shape[0])], axis=1)

    taken = (column(row_of(send[...])) == iota((LANES, fibres), 1)) | (land_column == iota((LANES, fibres), 1))
    keep = jnp.max(jnp.where(taken, 1.0, 0.0), axis=0, keepdims=True) < 0.5
    hot_land[...] = onehot(land_column, iota((LANES, fibres), 1))
    kind[...] = contacts[2:3, :]
    lam_now = jnp.where(keep, warm[...], 0.0)
    lam[...] = lam_now

    slots = iota((fibres, LANES), 0)
    for pair in range(2):
        hot = jnp.concatenate([onehot(slots, near[2 * pair + i:2 * pair + i + 1, :]) for i in range(2)], axis=1)
        at = slice(pair * 256, pair * 256 + 256)
        near_warm = join(dot(split(warm[...], 3), hot), 3)
        near_state[0, :, at] = near_velocity[:, at] - near_warm
        near_state[1, :, at] = join(dot(split(gap[...], 3), hot), 3)
        near_state[2, :, at] = near_warm

    own_part(drift, lam, table, partial)


def own_part(drift, lam, table, partial):
    fibres = drift.shape[1]
    velocity = split(drift[...] + lam[...], 3)

    for start in range(0, partial.shape[1], CHUNK):
        at = slice(start, start + CHUNK)
        partial[:, at] = join(dot(velocity, table[:fibres, at]), 3)


def rate_body(partial, extra, table, base, stacked, kind_row, rate_out):
    width, count = partial.shape
    kinds = stacked.shape[1] // width
    rows = extra.shape[1]
    for start in range(0, count, RATE_SIZE):
        at = slice(start, start + RATE_SIZE)
        far = join(dot(extra[...], table[base:base + rows, at]), 3)
        diff = (partial[:, at] + far).astype(BF16)
        kind = kind_row[:, at]
        none = jnp.zeros_like(diff)
        chosen = jnp.concatenate([jnp.where(kind == i, diff, none) for i in range(kinds)], axis=0)
        rate_out[:, at] = split(dot(stacked[...], chosen), 2)


def near_update(near_in, near_state, near_lam, rate, hot_near, outs):
    faces = []
    for pair in range(2):
        at = slice(pair * 256, pair * 256 + 256)
        rates = join(dot(rate[...], hot_near[:, at]), 2)
        lam = project(near_in[:, at] - OMEGA * (rates + near_state[1, :, at]))
        near_lam[:, at] = lam
        velocity = near_state[0, :, at] + lam
        faces += [velocity[:, i * LANES:(i + 1) * LANES] for i in range(2)]
    for out, block in zip(outs, outgoing(faces)):
        out[...] = block


def first_kernel(part0, part1, part2, part3, hot_land, lam_in, partial, table, stacked, kind,
                 hot_near, near_state, rate, near_lam, lam, out0, out1, out2, out3, extra):
    width, fibres = lam_in.shape
    quarter = width // 4
    parts = (part0, part1, part2, part3)
    blocks = incoming([part[:width, :] for part in parts], CHIP_LAST)
    packed = incoming([part[width:, :] for part in parts], CHIP_LAST)
    group = lane_group(quarter)
    arrived = []
    for q in range(4):
        block = jnp.zeros((quarter, LANES), F32)
        for face in range(4):
            rows = packed[face]
            moved = pltpu.roll(rows, (32 * (face - q)) % LANES, 1) if q != face else rows
            block = jnp.where(group == face, moved, block)
        arrived.append(block)
    arrived = jnp.concatenate(arrived, axis=0)
    near = len(blocks) * LANES
    for i, block in enumerate(blocks + [arrived]):
        extra[:, i * LANES:(i + 1) * LANES] = split(block, 3)
    rate_body(partial, extra, table, fibres, stacked, kind, rate)
    near_update(near_state[2], near_state, near_lam, rate, hot_near, (out0, out1, out2, out3))
    lam[...] = lam_in[...] + join(dot(extra[:, near:], hot_land[...]), 3)


def sweep_kernel(part0, part1, part2, part3, partial, table, stacked, kind,
                 hot_near, near_state, near_in, rate, near_lam, out0, out1, out2, out3, extra):
    parts = [part[...] for part in (part0, part1, part2, part3)]
    for i, block in enumerate(incoming(parts, CHIP_LAST)):
        extra[:, i * LANES:(i + 1) * LANES] = split(block, 3)
    fibres = table.shape[0] - LANES - extra.shape[1]
    rate_body(partial, extra, table, fibres, stacked, kind, rate)
    near_update(near_in, near_state, near_lam, rate, hot_near, (out0, out1, out2, out3))


def update(rate, hot_first, lam_in, gap, lam, at, rates=None):
    total = join(dot(rate[...], hot_first[:, at]), 2)
    lam[:, at] = project(lam_in[:, at] - OMEGA * (total + gap[:, at]))
    if rates is not None:
        rates[:, at] = total


def own_kernel(rate, hot_first, lam_in, gap, drift, table, lam, partial):
    for start in range(0, lam.shape[1], CHUNK):
        update(rate, hot_first, lam_in, gap, lam, slice(start, start + CHUNK))
    own_part(drift, lam, table, partial)


def last_kernel(part0, part1, part2, part3, partial, table, stacked, kind,
                hot_first, lam_in, gap, lam_out, rates_out, rate, extra, lam, rates, sems):
    parts = [part[...] for part in (part0, part1, part2, part3)]
    for i, block in enumerate(incoming(parts, CHIP_FIRST)):
        extra[:, i * LANES:(i + 1) * LANES] = split(block, 3)
    fibres = table.shape[0] - LANES - extra.shape[1]
    rate_body(partial, extra, table, fibres, stacked, kind, rate)
    copies = []
    for n, start in enumerate(range(0, lam.shape[1], CHUNK)):
        at = slice(start, start + CHUNK)
        update(rate, hot_first, lam_in, gap, lam, at, rates)
        for i, (source, target) in enumerate(((lam, lam_out), (rates, rates_out))):
            copy = pltpu.make_async_copy(source.at[:, at], target.at[:, at], sems.at[n, i])
            copy.start()
            copies.append(copy)
    for copy in copies:
        copy.wait()


def call(kernel, outs, args, scalars=0, scratch=(), flops=0, space=pltpu.VMEM, out_space=pltpu.VMEM):
    scalar = pl.BlockSpec(memory_space=pltpu.SMEM)
    return pl.pallas_call(
        kernel,
        out_shape=[jax.ShapeDtypeStruct(s, d) for s, d in outs],
        in_specs=[scalar] * scalars + [pl.BlockSpec(memory_space=space)] * (len(args) - scalars),
        out_specs=[pl.BlockSpec(memory_space=out_space)] * len(outs),
        scratch_shapes=list(scratch),
        compiler_params=pltpu.CompilerParams(vmem_limit_bytes=VMEM_LIMIT),
        cost_estimate=pl.CostEstimate(flops=flops, bytes_accessed=4 << 20, transcendentals=0),
    )(*args)


def per_device(drift, warm, gap, mobility, near_list, send_slot, land_slot, contacts, live):
    width, fibres = drift.shape[0] * drift.shape[1], drift.shape[2]
    count = contacts.shape[1]
    near = near_list.shape[0] * near_list.shape[1]
    shape = drift.shape
    drift, warm, gap = (x.reshape(width, fibres) for x in (drift, warm, gap))
    total = fibres + near + LANES
    face = ((width, LANES), F32)
    big = ((width, fibres), F32)
    rate_shape = ((2 * width, count), BF16)
    near_shape = ((width, near), F32)
    partial_shape = ((width, count), F32)

    held = [pltpu.with_memory_space_constraint(x, pltpu.HBM) for x in (drift, warm, near_list, send_slot)]
    *sent, near_velocity = call(
        send_kernel, [((width + width // 4, LANES), F32)] * 4 + [near_shape], held, flops=2 << 30, space=pltpu.HBM,
        scratch=[pltpu.VMEM(x.shape, x.dtype) for x in held] + [pltpu.SemaphoreType.DMA((len(held),)), pltpu.VMEM((fibres, near), BF16), pltpu.VMEM((fibres, LANES), BF16)])
    halo = exchange(sent, CHIP_LAST)
    table, hot_first, hot_near, hot_land, kind, partial, lam, near_state, stacked = call(
        setup_kernel,
        [((total, count), BF16), ((count, fibres), BF16), ((count, near), BF16), ((LANES, fibres), BF16),
         ((1, count), jnp.int32), partial_shape, big, ((3, width, near), F32),
         ((width, mobility.shape[0] * width), BF16)],
        (live, drift, warm, gap, near_list, send_slot, land_slot, contacts, mobility, near_velocity), scalars=1,
        flops=8 << 30)
    rate, near_lam, lam, *sent = call(
        first_kernel, [rate_shape, near_shape, big] + [face] * 4,
        (*halo, hot_land, lam, partial, table, stacked, kind, hot_near, near_state),
        scratch=[pltpu.VMEM((3 * width, near + LANES), BF16)], flops=4 << 30)
    for repeat in range(1, SWEEPS):
        halo = exchange(sent, CHIP_LAST if repeat < SWEEPS - 1 else CHIP_FIRST)
        lam, partial = call(own_kernel, [big, partial_shape], (rate, hot_first, lam, gap, drift, table),
                            flops=8 << 30)
        extra = pltpu.VMEM((3 * width, near), BF16)
        if repeat < SWEEPS - 1:
            rate, near_lam, *sent = call(
                sweep_kernel, [rate_shape, near_shape] + [face] * 4,
                (*halo, partial, table, stacked, kind, hot_near, near_state, near_lam),
                scratch=[extra], flops=4 << 30)
    lam, rates = call(
        last_kernel, [big, big],
        (*halo, partial, table, stacked, kind, hot_first, lam, gap),
        scratch=[pltpu.VMEM(*rate_shape), extra, pltpu.VMEM(*big), pltpu.VMEM(*big),
                 pltpu.SemaphoreType.DMA((fibres // CHUNK, 2))], flops=4 << 30, out_space=pltpu.HBM)
    return lam.reshape(shape), rates.reshape(shape)


def solution(mesh):
    both = ("grav", "cross")
    return jax.shard_map(
        per_device,
        mesh=mesh,
        in_specs=(
            P(None, None, both),
            P(None, None, both),
            P(None, None, both),
            P(),
            P(None, both),
            P(None, both),
            P(None, both),
            P(None, both),
            P(both),
        ),
        out_specs=(P(None, None, both), P(None, None, both)),
        check_vma=False,
    )
```

```python
import functools

import jax
import jax.numpy as jnp
from jax import lax
from jax.experimental import pallas as pl
from jax.experimental.pallas import tpu as pltpu
from jax.sharding import PartitionSpec as P

SWEEPS = 3
OMEGA = 0.5
FRICTION = 0.4
LANES = 128
CHUNK = 256
RATE_SIZE = 1024
VMEM_LIMIT = 24 * 1024 * 1024
F32 = jnp.float32
BF16 = jnp.bfloat16


def swap(x, axis, offset):
    count = lax.axis_size(axis)
    pairs = []
    for low in range(offset, count, 2):
        high = (low + 1) % count
        pairs += [(low, high), (high, low)]
    return lax.ppermute(x, axis, pairs)


STEPS = (("cross", 1), ("grav", 0), ("grav", 1), ("cross", 0))
CHIP_FIRST = (3, 0, 1, 2)
CHIP_LAST = (0, 1, 2, 3)


def exchange(sent, order):
    return [swap(sent[step], *STEPS[step]) for step in order]


def odd(axis):
    return lax.rem(lax.axis_index(axis), 2) == 1


def outgoing(faces):
    c, g = odd("cross"), odd("grav")
    return (jnp.where(c, faces[3], faces[2]), jnp.where(g, faces[0], faces[1]),
            jnp.where(g, faces[1], faces[0]), jnp.where(c, faces[2], faces[3]))


def incoming(parts, order):
    parts = [parts[order.index(step)] for step in range(len(order))]
    c, g = odd("cross"), odd("grav")
    place = lax.axis_index("grav")
    below, above = jnp.where(g, parts[1], parts[2]), jnp.where(g, parts[2], parts[1])
    return [jnp.where(place == 0, 0.0, below), jnp.where(place == lax.axis_size("grav") - 1, 0.0, above),
            jnp.where(c, parts[3], parts[0]), jnp.where(c, parts[0], parts[3])]


def split(x, parts):
    out = []
    for _ in range(parts - 1):
        part = x.astype(BF16)
        out.append(part)
        x = x - part.astype(F32)
    out.append(x.astype(BF16))
    return jnp.concatenate(out, axis=0)


def join(y, parts):
    rows = y.shape[0] // parts
    total = y[(parts - 1) * rows:]
    for i in range(parts - 2, -1, -1):
        total = total + y[i * rows:(i + 1) * rows]
    return total


def dot(a, b):
    return jnp.dot(a, b, preferred_element_type=F32)


def iota(shape, dim):
    return lax.broadcasted_iota(jnp.int32, shape, dim)


def narrow(x, shape):
    return jnp.broadcast_to(x, shape).astype(jnp.int16)


def onehot(ids, wanted):
    shape = jnp.broadcast_shapes(ids.shape, wanted.shape)
    one, zero = jnp.ones(shape, BF16), jnp.zeros(shape, BF16)
    return jnp.where(narrow(ids, shape) == narrow(wanted, shape), one, zero)


def signed(ids, first, second):
    shape = jnp.broadcast_shapes(ids.shape, first.shape)
    one, zero = jnp.ones(shape, BF16), jnp.zeros(shape, BF16)
    ids = narrow(ids, shape)
    return jnp.where(ids == narrow(first, shape), one, jnp.where(ids == narrow(second, shape), -one, zero))


def column(row):
    size = row.shape[1]
    eye = iota((size, size), 0) == iota((size, size), 1)
    return jnp.sum(jnp.where(eye, row.astype(F32), 0.0), axis=1, keepdims=True).astype(jnp.int32)


def row_of(table):
    return jnp.concatenate([table[i:i + 1] for i in range(table.shape[0])], axis=1)


def project(trial):
    third = trial.shape[0] // 3
    normal = jnp.maximum(trial[:third], 0.0)
    bound = FRICTION * normal
    first = jnp.minimum(jnp.maximum(trial[third:2 * third], -bound), bound)
    second = jnp.minimum(jnp.maximum(trial[2 * third:], -bound), bound)
    return jnp.concatenate([normal, first, second], axis=0)


def lane_group(rows):
    return iota((rows, LANES), 1) // 32


def send_kernel(drift_hbm, warm_hbm, near_hbm, send_hbm, out0, out1, out2, out3, velocity_out,
                drift, warm, near, send, sems, hot_near, hot_send):
    copies = [pltpu.make_async_copy(source, target, sems.at[i]) for i, (source, target) in enumerate(
        ((near_hbm, near), (send_hbm, send), (warm_hbm, warm), (drift_hbm, drift)))]
    for copy in copies:
        copy.start()
    width, fibres = drift.shape
    quarter = width // 4
    slots = iota((fibres, LANES), 0)
    copies[0].wait()
    for face in range(4):
        hot_near[:, face * LANES:(face + 1) * LANES] = onehot(slots, near[face:face + 1, :])
    copies[1].wait()
    hot_send[...] = onehot(slots, row_of(send[...]))
    copies[2].wait()
    warm_now = warm[...]
    leaving = join(dot(split(warm_now, 3), hot_send[...]), 3)
    copies[3].wait()
    velocity = split(drift[...] + warm_now, 3)
    group = lane_group(quarter)
    blocks = []
    for pair in range(2):
        picked = join(dot(velocity, hot_near[:, pair * 256:pair * 256 + 256]), 3)
        velocity_out[:, pair * 256:pair * 256 + 256] = picked
        for i in range(2):
            face = 2 * pair + i
            packed = jnp.zeros((quarter, LANES), F32)
            for q in range(4):
                rows = leaving[q * quarter:(q + 1) * quarter]
                moved = pltpu.roll(rows, (32 * (q - face)) % LANES, 1) if q != face else rows
                packed = jnp.where(group == q, moved, packed)
            blocks.append((picked[:, i * LANES:(i + 1) * LANES], packed))
    for out, block, packed in zip((out0, out1, out2, out3), outgoing([b[0] for b in blocks]),
                                  outgoing([b[1] for b in blocks])):
        out[:width, :] = block
        out[width:, :] = packed


def setup_kernel(live, drift, warm, gap, near, send, land, contacts, mobility, near_velocity,
                 table, hot_near, hot_land, kind, partial, lam, near_state, stacked):
    width, fibres = drift.shape
    count = contacts.shape[1]
    total = table.shape[0]

    land_row = row_of(land[...])
    land_column = column(land_row)

    for start in range(0, count, CHUNK):
        at = slice(start, start + CHUNK)
        alive = start + iota((1, CHUNK), 1) < live[0]
        first = jnp.where(alive, contacts[0:1, at], -1)
        second = jnp.where(alive, contacts[1:2, at], -1)
        for row in range(0, total - LANES, LANES):
            table[row:row + LANES, at] = signed(row + iota((LANES, CHUNK), 0), first, second)
        table[total - LANES:, at] = signed(land_column, first, second)

    for start in range(0, count, LANES):
        at = slice(start, start + LANES)
        first = column(contacts[0:1, at])
        for face in range(4):
            hot_near[at, face * LANES:(face + 1) * LANES] = onehot(first, near[face:face + 1, :])

    stacked[...] = jnp.concatenate([mobility[i] for i in range(mobility.shape[0])], axis=1)

    taken = (column(row_of(send[...])) == iota((LANES, fibres), 1)) | (land_column == iota((LANES, fibres), 1))
    keep = jnp.max(jnp.where(taken, 1.0, 0.0), axis=0, keepdims=True) < 0.5
    hot_land[...] = onehot(land_column, iota((LANES, fibres), 1))
    kind[...] = contacts[2:3, :]
    lam_now = jnp.where(keep, warm[...], 0.0)
    lam[...] = lam_now

    slots = iota((fibres, LANES), 0)
    for pair in range(2):
        hot = jnp.concatenate([onehot(slots, near[2 * pair + i:2 * pair + i + 1, :]) for i in range(2)], axis=1)
        at = slice(pair * 256, pair * 256 + 256)
        near_warm = join(dot(split(warm[...], 3), hot), 3)
        near_state[0, :, at] = near_velocity[:, at] - near_warm
        near_state[1, :, at] = join(dot(split(gap[...], 3), hot), 3)
        near_state[2, :, at] = near_warm

    own_part(drift, lam, table, partial)


def own_part(drift, lam, table, partial):
    fibres = drift.shape[1]
    velocity = split(drift[...] + lam[...], 3)

    for start in range(0, partial.shape[1], CHUNK):
        at = slice(start, start + CHUNK)
        partial[:, at] = join(dot(velocity, table[:fibres, at]), 3)


def rate_body(partial, extra, table, base, stacked, kind_row, rate_out):
    width, count = partial.shape
    kinds = stacked.shape[1] // width
    rows = extra.shape[1]
    for start in range(0, count, RATE_SIZE):
        at = slice(start, start + RATE_SIZE)
        far = join(dot(extra[...], table[base:base + rows, at]), 3)
        diff = (partial[:, at] + far).astype(BF16)
        kind = kind_row[:, at]
        none = jnp.zeros_like(diff)
        chosen = jnp.concatenate([jnp.where(kind == i, diff, none) for i in range(kinds)], axis=0)
        rate_out[:, at] = split(dot(stacked[...], chosen), 2)


def near_update(near_in, near_state, near_lam, rate, hot_near, outs):
    faces = []
    for pair in range(2):
        at = slice(pair * 256, pair * 256 + 256)
        rates = join(dot(rate[...], hot_near[:, at]), 2)
        lam = project(near_in[:, at] - OMEGA * (rates + near_state[1, :, at]))
        near_lam[:, at] = lam
        velocity = near_state[0, :, at] + lam
        faces += [velocity[:, i * LANES:(i + 1) * LANES] for i in range(2)]
    for out, block in zip(outs, outgoing(faces)):
        out[...] = block


def first_kernel(part0, part1, part2, part3, partial, table, stacked, kind,
                 hot_near, near_state, rate, near_lam, landed, out0, out1, out2, out3, extra):
    width = partial.shape[0]
    fibres = table.shape[0] - hot_near.shape[1] - LANES
    quarter = width // 4
    parts = (part0, part1, part2, part3)
    blocks = incoming([part[:width, :] for part in parts], CHIP_LAST)
    packed = incoming([part[width:, :] for part in parts], CHIP_LAST)
    group = lane_group(quarter)
    arrived = []
    for q in range(4):
        block = jnp.zeros((quarter, LANES), F32)
        for face in range(4):
            rows = packed[face]
            moved = pltpu.roll(rows, (32 * (face - q)) % LANES, 1) if q != face else rows
            block = jnp.where(group == face, moved, block)
        arrived.append(block)
    arrived = jnp.concatenate(arrived, axis=0)
    near = len(blocks) * LANES
    for i, block in enumerate(blocks + [arrived]):
        extra[:, i * LANES:(i + 1) * LANES] = split(block, 3)
    rate_body(partial, extra, table, fibres, stacked, kind, rate)
    near_update(near_state[2], near_state, near_lam, rate, hot_near, (out0, out1, out2, out3))
    landed[...] = arrived


def sweep_kernel(part0, part1, part2, part3, partial, table, stacked, kind,
                 hot_near, near_state, near_in, rate, near_lam, out0, out1, out2, out3, extra):
    parts = [part[...] for part in (part0, part1, part2, part3)]
    for i, block in enumerate(incoming(parts, CHIP_LAST)):
        extra[:, i * LANES:(i + 1) * LANES] = split(block, 3)
    fibres = table.shape[0] - LANES - extra.shape[1]
    rate_body(partial, extra, table, fibres, stacked, kind, rate)
    near_update(near_in, near_state, near_lam, rate, hot_near, (out0, out1, out2, out3))


def update(rate, hot_first, lam_in, gap, lam, at, rates=None):
    total = join(dot(rate[...], hot_first[:, at]), 2)
    lam[:, at] = project(lam_in[:, at] - OMEGA * (total + gap[:, at]))
    if rates is not None:
        rates[:, at] = total


def own_first_kernel(rate, contacts, landed, hot_land, lam_in, gap, drift, table, lam, partial, hot_first):
    arrived = split(landed[...], 3)
    firsts = [column(contacts[0:1, start:start + LANES]) for start in range(0, contacts.shape[1], LANES)]
    for start in range(0, lam.shape[1], CHUNK):
        at = slice(start, start + CHUNK)
        for i, first in enumerate(firsts):
            hot_first[i * LANES:(i + 1) * LANES, at] = onehot(first, start + iota((LANES, CHUNK), 1))
        before = lam_in[:, at] + join(dot(arrived, hot_land[:, at]), 3)
        total = join(dot(rate[...], hot_first[:, at]), 2)
        lam[:, at] = project(before - OMEGA * (total + gap[:, at]))
    own_part(drift, lam, table, partial)


def own_kernel(rate, hot_first, lam_in, gap, drift, table, lam, partial):
    for start in range(0, lam.shape[1], CHUNK):
        update(rate, hot_first, lam_in, gap, lam, slice(start, start + CHUNK))
    own_part(drift, lam, table, partial)


def last_kernel(part0, part1, part2, part3, partial, table, stacked, kind,
                hot_first, lam_in, gap, lam_out, rates_out, rate, extra, lam, rates, sems):
    parts = [part[...] for part in (part0, part1, part2, part3)]
    for i, block in enumerate(incoming(parts, CHIP_FIRST)):
        extra[:, i * LANES:(i + 1) * LANES] = split(block, 3)
    fibres = table.shape[0] - LANES - extra.shape[1]
    rate_body(partial, extra, table, fibres, stacked, kind, rate)
    copies = []
    for n, start in enumerate(range(0, lam.shape[1], CHUNK)):
        at = slice(start, start + CHUNK)
        update(rate, hot_first, lam_in, gap, lam, at, rates)
        for i, (source, target) in enumerate(((lam, lam_out), (rates, rates_out))):
            copy = pltpu.make_async_copy(source.at[:, at], target.at[:, at], sems.at[n, i])
            copy.start()
            copies.append(copy)
    for copy in copies:
        copy.wait()


def call(kernel, outs, args, scalars=0, scratch=(), flops=0, space=pltpu.VMEM, out_space=pltpu.VMEM):
    scalar = pl.BlockSpec(memory_space=pltpu.SMEM)
    return pl.pallas_call(
        kernel,
        out_shape=[jax.ShapeDtypeStruct(s, d) for s, d in outs],
        in_specs=[scalar] * scalars + [pl.BlockSpec(memory_space=space)] * (len(args) - scalars),
        out_specs=[pl.BlockSpec(memory_space=out_space)] * len(outs),
        scratch_shapes=list(scratch),
        compiler_params=pltpu.CompilerParams(vmem_limit_bytes=VMEM_LIMIT),
        cost_estimate=pl.CostEstimate(flops=flops, bytes_accessed=4 << 20, transcendentals=0),
    )(*args)


def per_device(drift, warm, gap, mobility, near_list, send_slot, land_slot, contacts, live):
    width, fibres = drift.shape[0] * drift.shape[1], drift.shape[2]
    count = contacts.shape[1]
    near = near_list.shape[0] * near_list.shape[1]
    shape = drift.shape
    drift, warm, gap = (x.reshape(width, fibres) for x in (drift, warm, gap))
    total = fibres + near + LANES
    face = ((width, LANES), F32)
    big = ((width, fibres), F32)
    rate_shape = ((2 * width, count), BF16)
    near_shape = ((width, near), F32)
    partial_shape = ((width, count), F32)

    held = [pltpu.with_memory_space_constraint(x, pltpu.HBM) for x in (drift, warm, near_list, send_slot)]
    *sent, near_velocity = call(
        send_kernel, [((width + width // 4, LANES), F32)] * 4 + [near_shape], held, flops=2 << 30, space=pltpu.HBM,
        scratch=[pltpu.VMEM(x.shape, x.dtype) for x in held] + [pltpu.SemaphoreType.DMA((len(held),)), pltpu.VMEM((fibres, near), BF16), pltpu.VMEM((fibres, LANES), BF16)])
    halo = exchange(sent, CHIP_LAST)
    table, hot_near, hot_land, kind, partial, lam, near_state, stacked = call(
        setup_kernel,
        [((total, count), BF16), ((count, near), BF16), ((LANES, fibres), BF16),
         ((1, count), jnp.int32), partial_shape, big, ((3, width, near), F32),
         ((width, mobility.shape[0] * width), BF16)],
        (live, drift, warm, gap, near_list, send_slot, land_slot, contacts, mobility, near_velocity), scalars=1,
        flops=8 << 30)
    rate, near_lam, landed, *sent = call(
        first_kernel, [rate_shape, near_shape, face] + [face] * 4,
        (*halo, partial, table, stacked, kind, hot_near, near_state),
        scratch=[pltpu.VMEM((3 * width, near + LANES), BF16)], flops=4 << 30)
    for repeat in range(1, SWEEPS):
        halo = exchange(sent, CHIP_LAST if repeat < SWEEPS - 1 else CHIP_FIRST)
        if repeat == 1:
            lam, partial, hot_first = call(
                own_first_kernel, [big, partial_shape, ((count, fibres), BF16)],
                (rate, contacts, landed, hot_land, lam, gap, drift, table), flops=8 << 30)
        else:
            lam, partial = call(own_kernel, [big, partial_shape], (rate, hot_first, lam, gap, drift, table),
                                flops=8 << 30)
        extra = pltpu.VMEM((3 * width, near), BF16)
        if repeat < SWEEPS - 1:
            rate, near_lam, *sent = call(
                sweep_kernel, [rate_shape, near_shape] + [face] * 4,
                (*halo, partial, table, stacked, kind, hot_near, near_state, near_lam),
                scratch=[extra], flops=4 << 30)
    lam, rates = call(
        last_kernel, [big, big],
        (*halo, partial, table, stacked, kind, hot_first, lam, gap),
        scratch=[pltpu.VMEM(*rate_shape), extra, pltpu.VMEM(*big), pltpu.VMEM(*big),
                 pltpu.SemaphoreType.DMA((fibres // CHUNK, 2))], flops=4 << 30, out_space=pltpu.HBM)
    return lam.reshape(shape), rates.reshape(shape)


def solution(mesh):
    both = ("grav", "cross")
    return jax.shard_map(
        per_device,
        mesh=mesh,
        in_specs=(
            P(None, None, both),
            P(None, None, both),
            P(None, None, both),
            P(),
            P(None, both),
            P(None, both),
            P(None, both),
            P(None, both),
            P(both),
        ),
        out_specs=(P(None, None, both), P(None, None, both)),
        check_vma=False,
    )
```

```python
import functools

import jax
import jax.numpy as jnp
from jax import lax
from jax.experimental import pallas as pl
from jax.experimental.pallas import tpu as pltpu
from jax.sharding import PartitionSpec as P

SWEEPS = 3
OMEGA = 0.5
FRICTION = 0.4
LANES = 128
CHUNK = 256
RATE_SIZE = 1024
VMEM_LIMIT = 24 * 1024 * 1024
F32 = jnp.float32
BF16 = jnp.bfloat16


def swap(x, axis, offset):
    count = lax.axis_size(axis)
    pairs = []
    for low in range(offset, count, 2):
        high = (low + 1) % count
        pairs += [(low, high), (high, low)]
    return lax.ppermute(x, axis, pairs)


STEPS = (("cross", 1), ("grav", 0), ("grav", 1), ("cross", 0))
CHIP_FIRST = (3, 0, 2, 1)
CHIP_LAST = (0, 2, 1, 3)


def exchange(sent, order):
    return [swap(sent[step], *STEPS[step]) for step in order]


def odd(axis):
    return lax.rem(lax.axis_index(axis), 2) == 1


def outgoing(faces):
    c, g = odd("cross"), odd("grav")
    return (jnp.where(c, faces[3], faces[2]), jnp.where(g, faces[0], faces[1]),
            jnp.where(g, faces[1], faces[0]), jnp.where(c, faces[2], faces[3]))


def incoming(parts, order):
    parts = [parts[order.index(step)] for step in range(len(order))]
    c, g = odd("cross"), odd("grav")
    place = lax.axis_index("grav")
    below, above = jnp.where(g, parts[1], parts[2]), jnp.where(g, parts[2], parts[1])
    return [jnp.where(place == 0, 0.0, below), jnp.where(place == lax.axis_size("grav") - 1, 0.0, above),
            jnp.where(c, parts[3], parts[0]), jnp.where(c, parts[0], parts[3])]


def split(x, parts):
    out = []
    for _ in range(parts - 1):
        part = x.astype(BF16)
        out.append(part)
        x = x - part.astype(F32)
    out.append(x.astype(BF16))
    return jnp.concatenate(out, axis=0)


def join(y, parts):
    rows = y.shape[0] // parts
    total = y[(parts - 1) * rows:]
    for i in range(parts - 2, -1, -1):
        total = total + y[i * rows:(i + 1) * rows]
    return total


def dot(a, b):
    return jnp.dot(a, b, preferred_element_type=F32)


def iota(shape, dim):
    return lax.broadcasted_iota(jnp.int32, shape, dim)


def narrow(x, shape):
    return jnp.broadcast_to(x, shape).astype(jnp.int16)


def onehot(ids, wanted):
    shape = jnp.broadcast_shapes(ids.shape, wanted.shape)
    one, zero = jnp.ones(shape, BF16), jnp.zeros(shape, BF16)
    return jnp.where(narrow(ids, shape) == narrow(wanted, shape), one, zero)


def signed(ids, first, second):
    shape = jnp.broadcast_shapes(ids.shape, first.shape)
    one, zero = jnp.ones(shape, BF16), jnp.zeros(shape, BF16)
    ids = narrow(ids, shape)
    return jnp.where(ids == narrow(first, shape), one, jnp.where(ids == narrow(second, shape), -one, zero))


def column(row):
    size = row.shape[1]
    eye = iota((size, size), 0) == iota((size, size), 1)
    return jnp.sum(jnp.where(eye, row.astype(F32), 0.0), axis=1, keepdims=True).astype(jnp.int32)


def row_of(table):
    return jnp.concatenate([table[i:i + 1] for i in range(table.shape[0])], axis=1)


def project(trial):
    third = trial.shape[0] // 3
    normal = jnp.maximum(trial[:third], 0.0)
    bound = FRICTION * normal
    first = jnp.minimum(jnp.maximum(trial[third:2 * third], -bound), bound)
    second = jnp.minimum(jnp.maximum(trial[2 * third:], -bound), bound)
    return jnp.concatenate([normal, first, second], axis=0)


def lane_group(rows):
    return iota((rows, LANES), 1) // 32


def send_kernel(drift_hbm, warm_hbm, near_hbm, send_hbm, out0, out1, out2, out3, velocity_out,
                drift, warm, near, send, sems, hot_near, hot_send):
    copies = [pltpu.make_async_copy(source, target, sems.at[i]) for i, (source, target) in enumerate(
        ((near_hbm, near), (send_hbm, send), (warm_hbm, warm), (drift_hbm, drift)))]
    for copy in copies:
        copy.start()
    width, fibres = drift.shape
    quarter = width // 4
    slots = iota((fibres, LANES), 0)
    copies[0].wait()
    for face in range(4):
        hot_near[:, face * LANES:(face + 1) * LANES] = onehot(slots, near[face:face + 1, :])
    copies[1].wait()
    hot_send[...] = onehot(slots, row_of(send[...]))
    copies[2].wait()
    warm_now = warm[...]
    leaving = join(dot(split(warm_now, 3), hot_send[...]), 3)
    copies[3].wait()
    velocity = split(drift[...] + warm_now, 3)
    group = lane_group(quarter)
    blocks = []
    for pair in range(2):
        picked = join(dot(velocity, hot_near[:, pair * 256:pair * 256 + 256]), 3)
        velocity_out[:, pair * 256:pair * 256 + 256] = picked
        for i in range(2):
            face = 2 * pair + i
            packed = jnp.zeros((quarter, LANES), F32)
            for q in range(4):
                rows = leaving[q * quarter:(q + 1) * quarter]
                moved = pltpu.roll(rows, (32 * (q - face)) % LANES, 1) if q != face else rows
                packed = jnp.where(group == q, moved, packed)
            blocks.append((picked[:, i * LANES:(i + 1) * LANES], packed))
    for out, block, packed in zip((out0, out1, out2, out3), outgoing([b[0] for b in blocks]),
                                  outgoing([b[1] for b in blocks])):
        out[:width, :] = block
        out[width:, :] = packed


def setup_kernel(live, drift, warm, gap, near, send, land, contacts, mobility, near_velocity,
                 table, hot_near, hot_land, kind, partial, lam, near_state, stacked):
    width, fibres = drift.shape
    count = contacts.shape[1]
    total = table.shape[0]

    land_row = row_of(land[...])
    land_column = column(land_row)

    for start in range(0, count, CHUNK):
        at = slice(start, start + CHUNK)
        alive = start + iota((1, CHUNK), 1) < live[0]
        first = jnp.where(alive, contacts[0:1, at], -1)
        second = jnp.where(alive, contacts[1:2, at], -1)
        for row in range(0, total - LANES, LANES):
            table[row:row + LANES, at] = signed(row + iota((LANES, CHUNK), 0), first, second)
        table[total - LANES:, at] = signed(land_column, first, second)

    for start in range(0, count, LANES):
        at = slice(start, start + LANES)
        first = column(contacts[0:1, at])
        for face in range(4):
            hot_near[at, face * LANES:(face + 1) * LANES] = onehot(first, near[face:face + 1, :])

    stacked[...] = jnp.concatenate([mobility[i] for i in range(mobility.shape[0])], axis=1)

    taken = (column(row_of(send[...])) == iota((LANES, fibres), 1)) | (land_column == iota((LANES, fibres), 1))
    keep = jnp.max(jnp.where(taken, 1.0, 0.0), axis=0, keepdims=True) < 0.5
    hot_land[...] = onehot(land_column, iota((LANES, fibres), 1))
    kind[...] = contacts[2:3, :]
    lam_now = jnp.where(keep, warm[...], 0.0)
    lam[...] = lam_now

    slots = iota((fibres, LANES), 0)
    for pair in range(2):
        hot = jnp.concatenate([onehot(slots, near[2 * pair + i:2 * pair + i + 1, :]) for i in range(2)], axis=1)
        at = slice(pair * 256, pair * 256 + 256)
        near_warm = join(dot(split(warm[...], 3), hot), 3)
        near_state[0, :, at] = near_velocity[:, at] - near_warm
        near_state[1, :, at] = join(dot(split(gap[...], 3), hot), 3)
        near_state[2, :, at] = near_warm

    own_part(drift, lam, table, partial)


def own_part(drift, lam, table, partial):
    fibres = drift.shape[1]
    velocity = split(drift[...] + lam[...], 3)

    for start in range(0, partial.shape[1], CHUNK):
        at = slice(start, start + CHUNK)
        partial[:, at] = join(dot(velocity, table[:fibres, at]), 3)


def rate_body(partial, extra, table, base, stacked, kind_row, rate_out):
    width, count = partial.shape
    kinds = stacked.shape[1] // width
    rows = extra.shape[1]
    for start in range(0, count, RATE_SIZE):
        at = slice(start, start + RATE_SIZE)
        far = join(dot(extra[...], table[base:base + rows, at]), 3)
        diff = (partial[:, at] + far).astype(BF16)
        kind = kind_row[:, at]
        none = jnp.zeros_like(diff)
        chosen = jnp.concatenate([jnp.where(kind == i, diff, none) for i in range(kinds)], axis=0)
        rate_out[:, at] = split(dot(stacked[...], chosen), 2)


def near_update(near_in, near_state, near_lam, rate, hot_near, outs):
    faces = []
    for pair in range(2):
        at = slice(pair * 256, pair * 256 + 256)
        rates = join(dot(rate[...], hot_near[:, at]), 2)
        lam = project(near_in[:, at] - OMEGA * (rates + near_state[1, :, at]))
        near_lam[:, at] = lam
        velocity = near_state[0, :, at] + lam
        faces += [velocity[:, i * LANES:(i + 1) * LANES] for i in range(2)]
    for out, block in zip(outs, outgoing(faces)):
        out[...] = block


def first_kernel(part0, part1, part2, part3, partial, table, stacked, kind,
                 hot_near, near_state, rate, near_lam, landed, out0, out1, out2, out3, extra):
    width = partial.shape[0]
    fibres = table.shape[0] - hot_near.shape[1] - LANES
    quarter = width // 4
    parts = (part0, part1, part2, part3)
    blocks = incoming([part[:width, :] for part in parts], CHIP_LAST)
    packed = incoming([part[width:, :] for part in parts], CHIP_LAST)
    group = lane_group(quarter)
    arrived = []
    for q in range(4):
        block = jnp.zeros((quarter, LANES), F32)
        for face in range(4):
            rows = packed[face]
            moved = pltpu.roll(rows, (32 * (face - q)) % LANES, 1) if q != face else rows
            block = jnp.where(group == face, moved, block)
        arrived.append(block)
    arrived = jnp.concatenate(arrived, axis=0)
    near = len(blocks) * LANES
    for i, block in enumerate(blocks + [arrived]):
        extra[:, i * LANES:(i + 1) * LANES] = split(block, 3)
    rate_body(partial, extra, table, fibres, stacked, kind, rate)
    near_update(near_state[2], near_state, near_lam, rate, hot_near, (out0, out1, out2, out3))
    landed[...] = arrived


def sweep_kernel(part0, part1, part2, part3, partial, table, stacked, kind,
                 hot_near, near_state, near_in, rate, near_lam, out0, out1, out2, out3, extra):
    parts = [part[...] for part in (part0, part1, part2, part3)]
    for i, block in enumerate(incoming(parts, CHIP_LAST)):
        extra[:, i * LANES:(i + 1) * LANES] = split(block, 3)
    fibres = table.shape[0] - LANES - extra.shape[1]
    rate_body(partial, extra, table, fibres, stacked, kind, rate)
    near_update(near_in, near_state, near_lam, rate, hot_near, (out0, out1, out2, out3))


def update(rate, hot_first, lam_in, gap, lam, at, rates=None):
    total = join(dot(rate[...], hot_first[:, at]), 2)
    lam[:, at] = project(lam_in[:, at] - OMEGA * (total + gap[:, at]))
    if rates is not None:
        rates[:, at] = total


def own_first_kernel(rate, contacts, landed, hot_land, lam_in, gap, drift, table, lam, partial, hot_first):
    arrived = split(landed[...], 3)
    firsts = [column(contacts[0:1, start:start + LANES]) for start in range(0, contacts.shape[1], LANES)]
    for start in range(0, lam.shape[1], CHUNK):
        at = slice(start, start + CHUNK)
        for i, first in enumerate(firsts):
            hot_first[i * LANES:(i + 1) * LANES, at] = onehot(first, start + iota((LANES, CHUNK), 1))
        before = lam_in[:, at] + join(dot(arrived, hot_land[:, at]), 3)
        total = join(dot(rate[...], hot_first[:, at]), 2)
        lam[:, at] = project(before - OMEGA * (total + gap[:, at]))
    own_part(drift, lam, table, partial)


def own_kernel(rate, hot_first, lam_in, gap, drift, table, lam, partial):
    for start in range(0, lam.shape[1], CHUNK):
        update(rate, hot_first, lam_in, gap, lam, slice(start, start + CHUNK))
    own_part(drift, lam, table, partial)


def last_kernel(part0, part1, part2, part3, partial, table, stacked, kind,
                hot_first, lam_in, gap, lam_out, rates_out, rate, extra, lam, rates, sems):
    parts = [part[...] for part in (part0, part1, part2, part3)]
    for i, block in enumerate(incoming(parts, CHIP_FIRST)):
        extra[:, i * LANES:(i + 1) * LANES] = split(block, 3)
    fibres = table.shape[0] - LANES - extra.shape[1]
    rate_body(partial, extra, table, fibres, stacked, kind, rate)
    copies = []
    for n, start in enumerate(range(0, lam.shape[1], CHUNK)):
        at = slice(start, start + CHUNK)
        update(rate, hot_first, lam_in, gap, lam, at, rates)
        for i, (source, target) in enumerate(((lam, lam_out), (rates, rates_out))):
            copy = pltpu.make_async_copy(source.at[:, at], target.at[:, at], sems.at[n, i])
            copy.start()
            copies.append(copy)
    for copy in copies:
        copy.wait()


def call(kernel, outs, args, scalars=0, scratch=(), flops=0, space=pltpu.VMEM, out_space=pltpu.VMEM):
    scalar = pl.BlockSpec(memory_space=pltpu.SMEM)
    return pl.pallas_call(
        kernel,
        out_shape=[jax.ShapeDtypeStruct(s, d) for s, d in outs],
        in_specs=[scalar] * scalars + [pl.BlockSpec(memory_space=space)] * (len(args) - scalars),
        out_specs=[pl.BlockSpec(memory_space=out_space)] * len(outs),
        scratch_shapes=list(scratch),
        compiler_params=pltpu.CompilerParams(vmem_limit_bytes=VMEM_LIMIT),
        cost_estimate=pl.CostEstimate(flops=flops, bytes_accessed=4 << 20, transcendentals=0),
    )(*args)


def per_device(drift, warm, gap, mobility, near_list, send_slot, land_slot, contacts, live):
    width, fibres = drift.shape[0] * drift.shape[1], drift.shape[2]
    count = contacts.shape[1]
    near = near_list.shape[0] * near_list.shape[1]
    shape = drift.shape
    drift, warm, gap = (x.reshape(width, fibres) for x in (drift, warm, gap))
    total = fibres + near + LANES
    face = ((width, LANES), F32)
    big = ((width, fibres), F32)
    rate_shape = ((2 * width, count), BF16)
    near_shape = ((width, near), F32)
    partial_shape = ((width, count), F32)

    held = [pltpu.with_memory_space_constraint(x, pltpu.HBM) for x in (drift, warm, near_list, send_slot)]
    *sent, near_velocity = call(
        send_kernel, [((width + width // 4, LANES), F32)] * 4 + [near_shape], held, flops=2 << 30, space=pltpu.HBM,
        scratch=[pltpu.VMEM(x.shape, x.dtype) for x in held] + [pltpu.SemaphoreType.DMA((len(held),)), pltpu.VMEM((fibres, near), BF16), pltpu.VMEM((fibres, LANES), BF16)])
    halo = exchange(sent, CHIP_LAST)
    table, hot_near, hot_land, kind, partial, lam, near_state, stacked = call(
        setup_kernel,
        [((total, count), BF16), ((count, near), BF16), ((LANES, fibres), BF16),
         ((1, count), jnp.int32), partial_shape, big, ((3, width, near), F32),
         ((width, mobility.shape[0] * width), BF16)],
        (live, drift, warm, gap, near_list, send_slot, land_slot, contacts, mobility, near_velocity), scalars=1,
        flops=8 << 30)
    rate, near_lam, landed, *sent = call(
        first_kernel, [rate_shape, near_shape, face] + [face] * 4,
        (*halo, partial, table, stacked, kind, hot_near, near_state),
        scratch=[pltpu.VMEM((3 * width, near + LANES), BF16)], flops=4 << 30)
    for repeat in range(1, SWEEPS):
        halo = exchange(sent, CHIP_LAST if repeat < SWEEPS - 1 else CHIP_FIRST)
        if repeat == 1:
            lam, partial, hot_first = call(
                own_first_kernel, [big, partial_shape, ((count, fibres), BF16)],
                (rate, contacts, landed, hot_land, lam, gap, drift, table), flops=8 << 30)
        else:
            lam, partial = call(own_kernel, [big, partial_shape], (rate, hot_first, lam, gap, drift, table),
                                flops=8 << 30)
        extra = pltpu.VMEM((3 * width, near), BF16)
        if repeat < SWEEPS - 1:
            rate, near_lam, *sent = call(
                sweep_kernel, [rate_shape, near_shape] + [face] * 4,
                (*halo, partial, table, stacked, kind, hot_near, near_state, near_lam),
                scratch=[extra], flops=4 << 30)
    lam, rates = call(
        last_kernel, [big, big],
        (*halo, partial, table, stacked, kind, hot_first, lam, gap),
        scratch=[pltpu.VMEM(*rate_shape), extra, pltpu.VMEM(*big), pltpu.VMEM(*big),
                 pltpu.SemaphoreType.DMA((fibres // CHUNK, 2))], flops=4 << 30, out_space=pltpu.HBM)
    return lam.reshape(shape), rates.reshape(shape)


def solution(mesh):
    both = ("grav", "cross")
    return jax.shard_map(
        per_device,
        mesh=mesh,
        in_specs=(
            P(None, None, both),
            P(None, None, both),
            P(None, None, both),
            P(),
            P(None, both),
            P(None, both),
            P(None, both),
            P(None, both),
            P(both),
        ),
        out_specs=(P(None, None, both), P(None, None, both)),
        check_vma=False,
    )
```

```python
import functools

import jax
import jax.numpy as jnp
from jax import lax
from jax.experimental import pallas as pl
from jax.experimental.pallas import tpu as pltpu
from jax.sharding import PartitionSpec as P

SWEEPS = 3
OMEGA = 0.5
FRICTION = 0.4
LANES = 128
CHUNK = 256
RATE_SIZE = 1024
VMEM_LIMIT = 24 * 1024 * 1024
F32 = jnp.float32
BF16 = jnp.bfloat16


def swap(x, axis, offset):
    count = lax.axis_size(axis)
    pairs = []
    for low in range(offset, count, 2):
        high = (low + 1) % count
        pairs += [(low, high), (high, low)]
    return lax.ppermute(x, axis, pairs)


STEPS = (("cross", 1), ("grav", 0), ("grav", 1), ("cross", 0))
CHIP_FIRST = (3, 0, 2, 1)
CHIP_THIRD = (0, 2, 3, 1)


def exchange(sent, order):
    return [swap(sent[step], *STEPS[step]) for step in order]


def odd(axis):
    return lax.rem(lax.axis_index(axis), 2) == 1


def outgoing(faces):
    c, g = odd("cross"), odd("grav")
    return (jnp.where(c, faces[3], faces[2]), jnp.where(g, faces[0], faces[1]),
            jnp.where(g, faces[1], faces[0]), jnp.where(c, faces[2], faces[3]))


def incoming(parts, order):
    parts = [parts[order.index(step)] for step in range(len(order))]
    c, g = odd("cross"), odd("grav")
    place = lax.axis_index("grav")
    below, above = jnp.where(g, parts[1], parts[2]), jnp.where(g, parts[2], parts[1])
    return [jnp.where(place == 0, 0.0, below), jnp.where(place == lax.axis_size("grav") - 1, 0.0, above),
            jnp.where(c, parts[3], parts[0]), jnp.where(c, parts[0], parts[3])]


def split(x, parts):
    out = []
    for _ in range(parts - 1):
        part = x.astype(BF16)
        out.append(part)
        x = x - part.astype(F32)
    out.append(x.astype(BF16))
    return jnp.concatenate(out, axis=0)


def join(y, parts):
    rows = y.shape[0] // parts
    total = y[(parts - 1) * rows:]
    for i in range(parts - 2, -1, -1):
        total = total + y[i * rows:(i + 1) * rows]
    return total


def dot(a, b):
    return jnp.dot(a, b, preferred_element_type=F32)


def iota(shape, dim):
    return lax.broadcasted_iota(jnp.int32, shape, dim)


def narrow(x, shape):
    return jnp.broadcast_to(x, shape).astype(jnp.int16)


def onehot(ids, wanted):
    shape = jnp.broadcast_shapes(ids.shape, wanted.shape)
    one, zero = jnp.ones(shape, BF16), jnp.zeros(shape, BF16)
    return jnp.where(narrow(ids, shape) == narrow(wanted, shape), one, zero)


def signed(ids, first, second):
    shape = jnp.broadcast_shapes(ids.shape, first.shape)
    one, zero = jnp.ones(shape, BF16), jnp.zeros(shape, BF16)
    ids = narrow(ids, shape)
    return jnp.where(ids == narrow(first, shape), one, jnp.where(ids == narrow(second, shape), -one, zero))


def column(row):
    size = row.shape[1]
    eye = iota((size, size), 0) == iota((size, size), 1)
    return jnp.sum(jnp.where(eye, row.astype(F32), 0.0), axis=1, keepdims=True).astype(jnp.int32)


def row_of(table):
    return jnp.concatenate([table[i:i + 1] for i in range(table.shape[0])], axis=1)


def project(trial):
    third = trial.shape[0] // 3
    normal = jnp.maximum(trial[:third], 0.0)
    bound = FRICTION * normal
    first = jnp.minimum(jnp.maximum(trial[third:2 * third], -bound), bound)
    second = jnp.minimum(jnp.maximum(trial[2 * third:], -bound), bound)
    return jnp.concatenate([normal, first, second], axis=0)


def lane_group(rows):
    return iota((rows, LANES), 1) // 32


def send_kernel(drift_hbm, warm_hbm, near_hbm, send_hbm, out0, out1, out2, out3, velocity_out,
                drift, warm, near, send, sems, hot_near, hot_send):
    copies = [pltpu.make_async_copy(source, target, sems.at[i]) for i, (source, target) in enumerate(
        ((near_hbm, near), (send_hbm, send), (warm_hbm, warm), (drift_hbm, drift)))]
    for copy in copies:
        copy.start()
    width, fibres = drift.shape
    quarter = width // 4
    slots = iota((fibres, LANES), 0)
    copies[0].wait()
    for face in range(4):
        hot_near[:, face * LANES:(face + 1) * LANES] = onehot(slots, near[face:face + 1, :])
    copies[1].wait()
    hot_send[...] = onehot(slots, row_of(send[...]))
    copies[2].wait()
    warm_now = warm[...]
    leaving = join(dot(split(warm_now, 3), hot_send[...]), 3)
    copies[3].wait()
    velocity = split(drift[...] + warm_now, 3)
    group = lane_group(quarter)
    blocks = []
    for pair in range(2):
        picked = join(dot(velocity, hot_near[:, pair * 256:pair * 256 + 256]), 3)
        velocity_out[:, pair * 256:pair * 256 + 256] = picked
        for i in range(2):
            face = 2 * pair + i
            packed = jnp.zeros((quarter, LANES), F32)
            for q in range(4):
                rows = leaving[q * quarter:(q + 1) * quarter]
                moved = pltpu.roll(rows, (32 * (q - face)) % LANES, 1) if q != face else rows
                packed = jnp.where(group == q, moved, packed)
            blocks.append((picked[:, i * LANES:(i + 1) * LANES], packed))
    for out, block, packed in zip((out0, out1, out2, out3), outgoing([b[0] for b in blocks]),
                                  outgoing([b[1] for b in blocks])):
        out[:width, :] = block
        out[width:, :] = packed


def setup_kernel(live, drift, warm, gap, near, send, land, contacts, mobility, near_velocity,
                 table, hot_near, hot_land, kind, partial, lam, near_state, stacked):
    width, fibres = drift.shape
    count = contacts.shape[1]
    total = table.shape[0]

    land_row = row_of(land[...])
    land_column = column(land_row)

    for start in range(0, count, CHUNK):
        at = slice(start, start + CHUNK)
        alive = start + iota((1, CHUNK), 1) < live[0]
        first = jnp.where(alive, contacts[0:1, at], -1)
        second = jnp.where(alive, contacts[1:2, at], -1)
        for row in range(0, total - LANES, LANES):
            table[row:row + LANES, at] = signed(row + iota((LANES, CHUNK), 0), first, second)
        table[total - LANES:, at] = signed(land_column, first, second)

    for start in range(0, count, LANES):
        at = slice(start, start + LANES)
        first = column(contacts[0:1, at])
        for face in range(4):
            hot_near[at, face * LANES:(face + 1) * LANES] = onehot(first, near[face:face + 1, :])

    stacked[...] = jnp.concatenate([mobility[i] for i in range(mobility.shape[0])], axis=1)

    taken = (column(row_of(send[...])) == iota((LANES, fibres), 1)) | (land_column == iota((LANES, fibres), 1))
    keep = jnp.max(jnp.where(taken, 1.0, 0.0), axis=0, keepdims=True) < 0.5
    hot_land[...] = onehot(land_column, iota((LANES, fibres), 1))
    kind[...] = contacts[2:3, :]
    lam_now = jnp.where(keep, warm[...], 0.0)
    lam[...] = lam_now

    slots = iota((fibres, LANES), 0)
    for pair in range(2):
        hot = jnp.concatenate([onehot(slots, near[2 * pair + i:2 * pair + i + 1, :]) for i in range(2)], axis=1)
        at = slice(pair * 256, pair * 256 + 256)
        near_warm = join(dot(split(warm[...], 3), hot), 3)
        near_state[0, :, at] = near_velocity[:, at] - near_warm
        near_state[1, :, at] = join(dot(split(gap[...], 3), hot), 3)
        near_state[2, :, at] = near_warm

    own_part(drift, lam, table, partial)


def own_part(drift, lam, table, partial):
    fibres = drift.shape[1]
    velocity = split(drift[...] + lam[...], 3)

    for start in range(0, partial.shape[1], CHUNK):
        at = slice(start, start + CHUNK)
        partial[:, at] = join(dot(velocity, table[:fibres, at]), 3)


def rate_body(partial, extra, table, base, stacked, kind_row, rate_out):
    width, count = partial.shape
    kinds = stacked.shape[1] // width
    rows = extra.shape[1]
    for start in range(0, count, RATE_SIZE):
        at = slice(start, start + RATE_SIZE)
        far = join(dot(extra[...], table[base:base + rows, at]), 3)
        diff = (partial[:, at] + far).astype(BF16)
        kind = kind_row[:, at]
        none = jnp.zeros_like(diff)
        chosen = jnp.concatenate([jnp.where(kind == i, diff, none) for i in range(kinds)], axis=0)
        rate_out[:, at] = split(dot(stacked[...], chosen), 2)


def near_update(near_in, near_state, near_lam, rate, hot_near, outs):
    faces = []
    for pair in range(2):
        at = slice(pair * 256, pair * 256 + 256)
        rates = join(dot(rate[...], hot_near[:, at]), 2)
        lam = project(near_in[:, at] - OMEGA * (rates + near_state[1, :, at]))
        near_lam[:, at] = lam
        velocity = near_state[0, :, at] + lam
        faces += [velocity[:, i * LANES:(i + 1) * LANES] for i in range(2)]
    for out, block in zip(outs, outgoing(faces)):
        out[...] = block


def first_kernel(part0, part1, part2, part3, partial, table, stacked, kind,
                 hot_near, near_state, rate, near_lam, landed, out0, out1, out2, out3, extra):
    width = partial.shape[0]
    fibres = table.shape[0] - hot_near.shape[1] - LANES
    quarter = width // 4
    parts = (part0, part1, part2, part3)
    blocks = incoming([part[:width, :] for part in parts], CHIP_THIRD)
    packed = incoming([part[width:, :] for part in parts], CHIP_THIRD)
    group = lane_group(quarter)
    arrived = []
    for q in range(4):
        block = jnp.zeros((quarter, LANES), F32)
        for face in range(4):
            rows = packed[face]
            moved = pltpu.roll(rows, (32 * (face - q)) % LANES, 1) if q != face else rows
            block = jnp.where(group == face, moved, block)
        arrived.append(block)
    arrived = jnp.concatenate(arrived, axis=0)
    near = len(blocks) * LANES
    for i, block in enumerate(blocks + [arrived]):
        extra[:, i * LANES:(i + 1) * LANES] = split(block, 3)
    rate_body(partial, extra, table, fibres, stacked, kind, rate)
    near_update(near_state[2], near_state, near_lam, rate, hot_near, (out0, out1, out2, out3))
    landed[...] = arrived


def sweep_kernel(part0, part1, part2, part3, partial, table, stacked, kind,
                 hot_near, near_state, near_in, rate, near_lam, out0, out1, out2, out3, extra):
    parts = [part[...] for part in (part0, part1, part2, part3)]
    for i, block in enumerate(incoming(parts, CHIP_THIRD)):
        extra[:, i * LANES:(i + 1) * LANES] = split(block, 3)
    fibres = table.shape[0] - LANES - extra.shape[1]
    rate_body(partial, extra, table, fibres, stacked, kind, rate)
    near_update(near_in, near_state, near_lam, rate, hot_near, (out0, out1, out2, out3))


def update(rate, hot_first, lam_in, gap, lam, at, rates=None):
    total = join(dot(rate[...], hot_first[:, at]), 2)
    lam[:, at] = project(lam_in[:, at] - OMEGA * (total + gap[:, at]))
    if rates is not None:
        rates[:, at] = total


def own_first_kernel(rate, contacts, landed, hot_land, lam_in, gap, drift, table, lam, partial, hot_first):
    arrived = split(landed[...], 3)
    firsts = [column(contacts[0:1, start:start + LANES]) for start in range(0, contacts.shape[1], LANES)]
    for start in range(0, lam.shape[1], CHUNK):
        at = slice(start, start + CHUNK)
        for i, first in enumerate(firsts):
            hot_first[i * LANES:(i + 1) * LANES, at] = onehot(first, start + iota((LANES, CHUNK), 1))
        before = lam_in[:, at] + join(dot(arrived, hot_land[:, at]), 3)
        total = join(dot(rate[...], hot_first[:, at]), 2)
        lam[:, at] = project(before - OMEGA * (total + gap[:, at]))
    own_part(drift, lam, table, partial)


def own_kernel(rate, hot_first, lam_in, gap, drift, table, lam, partial):
    for start in range(0, lam.shape[1], CHUNK):
        update(rate, hot_first, lam_in, gap, lam, slice(start, start + CHUNK))
    own_part(drift, lam, table, partial)


def last_kernel(part0, part1, part2, part3, partial, table, stacked, kind,
                hot_first, lam_in, gap, lam_out, rates_out, rate, extra, lam, rates, sems):
    parts = [part[...] for part in (part0, part1, part2, part3)]
    for i, block in enumerate(incoming(parts, CHIP_FIRST)):
        extra[:, i * LANES:(i + 1) * LANES] = split(block, 3)
    fibres = table.shape[0] - LANES - extra.shape[1]
    rate_body(partial, extra, table, fibres, stacked, kind, rate)
    copies = []
    for n, start in enumerate(range(0, lam.shape[1], CHUNK)):
        at = slice(start, start + CHUNK)
        update(rate, hot_first, lam_in, gap, lam, at, rates)
        for i, (source, target) in enumerate(((lam, lam_out), (rates, rates_out))):
            copy = pltpu.make_async_copy(source.at[:, at], target.at[:, at], sems.at[n, i])
            copy.start()
            copies.append(copy)
    for copy in copies:
        copy.wait()


def call(kernel, outs, args, scalars=0, scratch=(), flops=0, space=pltpu.VMEM, out_space=pltpu.VMEM):
    scalar = pl.BlockSpec(memory_space=pltpu.SMEM)
    return pl.pallas_call(
        kernel,
        out_shape=[jax.ShapeDtypeStruct(s, d) for s, d in outs],
        in_specs=[scalar] * scalars + [pl.BlockSpec(memory_space=space)] * (len(args) - scalars),
        out_specs=[pl.BlockSpec(memory_space=out_space)] * len(outs),
        scratch_shapes=list(scratch),
        compiler_params=pltpu.CompilerParams(vmem_limit_bytes=VMEM_LIMIT),
        cost_estimate=pl.CostEstimate(flops=flops, bytes_accessed=4 << 20, transcendentals=0),
    )(*args)


def per_device(drift, warm, gap, mobility, near_list, send_slot, land_slot, contacts, live):
    width, fibres = drift.shape[0] * drift.shape[1], drift.shape[2]
    count = contacts.shape[1]
    near = near_list.shape[0] * near_list.shape[1]
    shape = drift.shape
    drift, warm, gap = (x.reshape(width, fibres) for x in (drift, warm, gap))
    total = fibres + near + LANES
    face = ((width, LANES), F32)
    big = ((width, fibres), F32)
    rate_shape = ((2 * width, count), BF16)
    near_shape = ((width, near), F32)
    partial_shape = ((width, count), F32)

    held = [pltpu.with_memory_space_constraint(x, pltpu.HBM) for x in (drift, warm, near_list, send_slot)]
    *sent, near_velocity = call(
        send_kernel, [((width + width // 4, LANES), F32)] * 4 + [near_shape], held, flops=2 << 30, space=pltpu.HBM,
        scratch=[pltpu.VMEM(x.shape, x.dtype) for x in held] + [pltpu.SemaphoreType.DMA((len(held),)), pltpu.VMEM((fibres, near), BF16), pltpu.VMEM((fibres, LANES), BF16)])
    halo = exchange(sent, CHIP_THIRD)
    table, hot_near, hot_land, kind, partial, lam, near_state, stacked = call(
        setup_kernel,
        [((total, count), BF16), ((count, near), BF16), ((LANES, fibres), BF16),
         ((1, count), jnp.int32), partial_shape, big, ((3, width, near), F32),
         ((width, mobility.shape[0] * width), BF16)],
        (live, drift, warm, gap, near_list, send_slot, land_slot, contacts, mobility, near_velocity), scalars=1,
        flops=8 << 30)
    rate, near_lam, landed, *sent = call(
        first_kernel, [rate_shape, near_shape, face] + [face] * 4,
        (*halo, partial, table, stacked, kind, hot_near, near_state),
        scratch=[pltpu.VMEM((3 * width, near + LANES), BF16)], flops=4 << 30)
    for repeat in range(1, SWEEPS):
        halo = exchange(sent, CHIP_THIRD if repeat < SWEEPS - 1 else CHIP_FIRST)
        if repeat == 1:
            lam, partial, hot_first = call(
                own_first_kernel, [big, partial_shape, ((count, fibres), BF16)],
                (rate, contacts, landed, hot_land, lam, gap, drift, table), flops=8 << 30)
        else:
            lam, partial = call(own_kernel, [big, partial_shape], (rate, hot_first, lam, gap, drift, table),
                                flops=8 << 30)
        extra = pltpu.VMEM((3 * width, near), BF16)
        if repeat < SWEEPS - 1:
            rate, near_lam, *sent = call(
                sweep_kernel, [rate_shape, near_shape] + [face] * 4,
                (*halo, partial, table, stacked, kind, hot_near, near_state, near_lam),
                scratch=[extra], flops=4 << 30)
    lam, rates = call(
        last_kernel, [big, big],
        (*halo, partial, table, stacked, kind, hot_first, lam, gap),
        scratch=[pltpu.VMEM(*rate_shape), extra, pltpu.VMEM(*big), pltpu.VMEM(*big),
                 pltpu.SemaphoreType.DMA((fibres // CHUNK, 2))], flops=4 << 30, out_space=pltpu.HBM)
    return lam.reshape(shape), rates.reshape(shape)


def solution(mesh):
    both = ("grav", "cross")
    return jax.shard_map(
        per_device,
        mesh=mesh,
        in_specs=(
            P(None, None, both),
            P(None, None, both),
            P(None, None, both),
            P(),
            P(None, both),
            P(None, both),
            P(None, both),
            P(None, both),
            P(both),
        ),
        out_specs=(P(None, None, both), P(None, None, both)),
        check_vma=False,
    )
```
